32 devices in a mesh: groups: 2 (over y), expert: 4 (over z), dp: 2 (over x), mp: 2 (over core).
Axes of the slice: x: 2, y: 2, z: 4, core: 2. Of those that a mesh axis runs over, the one named last changes fastest.
Arguments:
- tokens: bfloat16 [768, 4096], P(('groups', 'expert', 'dp', 'mp')), parts along dimension 0, may hold values from -6 to 6
- pseudo: bfloat16 [768, 8, 1536], P(('groups', 'expert', 'dp', 'mp')), parts along dimension 0, may hold values from -6 to 6
- assign: int32 [768, 8], P(('groups', 'expert', 'dp', 'mp')), parts along dimension 0, may hold values from 0 to 127, all different within a row; in each aligned block of 24 rows (0 to 23, 24 to 47, ...) at most 2 rows name the same one
- counts: int32 [8], P(('groups', 'expert')), parts along dimension 0, may hold values from 12 to 48
- basis_act: bfloat16 [8, 4096, 2048], P(('groups', 'expert'), 'dp', 'mp'), parts along dimension 0, may hold values from -0.09375 to 0.09375
- basis_grad: bfloat16 [8, 1536, 1536], P(('groups', 'expert'), 'dp', 'mp'), parts along dimension 0, may hold values from -0.15625 to 0.15625
- queries_act: bfloat16 [32, 4096], P('groups', 'dp'), parts along dimension 0, may hold values from -6 to 6
- queries_grad: bfloat16 [32, 1536], P('groups', 'dp'), parts along dimension 0, may hold values from -6 to 6
- query_expert: int32 [32, 1], P('groups'), parts along dimension 0, may hold values from 0 to 3; in each aligned block of 16 rows (0 to 15, 16 to 31, ...) at most 6 rows name the same one
Outputs:
- act_cov: bfloat16 [8, 4096, 4096], P(('groups', 'expert'), 'dp', 'mp'), parts along dimension 0
- grad_cov: bfloat16 [8, 1536, 1536], P(('groups', 'expert'), 'dp', 'mp'), parts along dimension 0
- rot_act: bfloat16 [32, 2048], P(('groups', 'expert', 'dp'), 'mp'), parts along dimension 0
- rot_grad: bfloat16 [32, 1536], P(('groups', 'expert', 'dp'), 'mp'), parts along dimension 0
The draws below stay inside these ranges and needn't reach their ends.
There are 2 independent parts, one for each index of `groups`. The reference program is written for one: setup_inputs(seed, part) draws one part's arguments, and reference() takes and returns one part's arrays. A program takes and returns all parts, laid end to end along the dimension named above; each array names one. Nothing has to cross between parts.
Inputs may be any that keep to these rules, and one draw needn't show every extreme that they name: `assign`: each token names 8 different experts; in each aligned block of 24 tokens (the tokens of one device) no expert is named by more than 2 tokens, a bound that some block reaches. `query_expert`: no expert is named by more than 6 query rows, a bound that some block reaches.
All inputs are finite; a program needn't handle non-finite values.
Results may differ from the reference program's by a relative error of at most 0.001.
Values may be sent and summed in bfloat16 or wider, within the bound.
No kernel may reach another device: no remote copies, remote signals or barrier semaphores. Data moves between devices by JAX's collectives and lax.ppermute only.
A program may use at most 64 MiB of HBM per device.

```python
import math
import jax
import jax.numpy as jnp
import numpy as np
from jax import lax

D = 4096
FF = 1536
ROUTED = 128
TOPK = 8
EIG = 2048
TOK_DEV = 24
CAP = 2
TOKENS = 384
EXPERTS = 4
NQ = 16
QCAP = 6


def with_ends(drawn, stream_key, smallest, largest):
    place = [jax.random.randint(jax.random.fold_in(stream_key, axis), (), 0, length) for axis, length in enumerate(drawn.shape)]
    widest = drawn.shape.index(max(drawn.shape))
    beside = place[:widest] + [(place[widest] + 1) % drawn.shape[widest]] + place[widest + 1:]
    return drawn.at[tuple(place)].set(smallest).at[tuple(beside)].set(largest)


def levels(stream_key, shape, cuts, low, high):
    loudness = 1.0
    for dim, parts in cuts:
        heights = jax.random.uniform(jax.random.fold_in(jax.random.fold_in(stream_key, 6), dim), (parts,), jnp.float32, low / len(cuts), high / len(cuts))
        loudness = loudness * jnp.repeat(jnp.exp(heights), shape[dim] // parts).reshape((-1,) + (1,) * (len(shape) - 1 - dim))
    return loudness


def deal_out(rng, own, number, rows, count, top, most, lean):
    ranking = jax.random.permutation(rng, count)
    crowded, ordinary = shares(count, rows * top, most, lean, True), shares(count, rows * top, most, lean, False)
    places = jnp.arange(count)

    def named(lengths, rotation):
        used = int((lengths > 0).sum())
        fixed = max(1, used // 4)
        passed = fixed + (places - fixed + rotation * (used - fixed)) % max(1, count - fixed)
        return jnp.zeros((count,), jnp.int32).at[ranking[jnp.where(places < fixed, places, passed)]].set(jnp.asarray(lengths, jnp.int32))

    lengths = jnp.where(number % 4 == 0, named(crowded, number // 4), named(ordinary, number - number // 4 - 1))
    mixed = jax.random.permutation(jax.random.fold_in(own, 3), count)
    donor, receiver = mixed[0:count // 2 * 2:2], mixed[1:count // 2 * 2:2]
    slack = jnp.minimum(lengths[donor] - 1, most - lengths[receiver]) // 2
    slack = jnp.where((donor == ranking[0]) | (receiver == ranking[0]) | (lengths[receiver] == 0), 0, jnp.maximum(slack, 0))
    passed = jax.random.randint(jax.random.fold_in(own, 4), (count // 2,), 0, 1 << 20) % (slack + 1)
    lengths = lengths.at[donor].add(-passed).at[receiver].add(passed)
    items = jnp.searchsorted(jnp.cumsum(lengths), jnp.arange(rows * top), side="right").astype(jnp.int32)
    table = items.reshape(top, rows).T
    table = table[jax.random.permutation(jax.random.fold_in(own, 1), rows)]
    rotation = jax.random.randint(jax.random.fold_in(own, 2), (rows, 1), 0, top)
    return jnp.take_along_axis(table, (jnp.arange(top)[None, :] + rotation) % top, axis=1)


def shares(amount, total, most, slope, full):
    portions = [(1 << 20) // math.isqrt(rank ** slope) + 1 for rank in range(1, amount + 1)]
    largest = most if full else min(most, max(-(-total // amount), total * portions[0] // sum(portions)))
    least = 1 if total - largest >= amount - 1 else 0
    given, spare = [largest] + [least] * (amount - 1), total - largest - least * (amount - 1)
    while spare > 0:
        movable = [i for i in range(1, amount) if given[i] < largest] or [i for i in range(1, amount) if given[i] < most]
        pool, left = sum([portions[i] for i in movable]), spare
        for i in movable:
            addition = min(most - given[i], max(1, left * portions[i] // pool), spare)
            given[i] = given[i] + addition
            spare = spare - addition
    return np.array(given)


def noise(rng, dims, width, bound, cuts=(), held_as=jnp.bfloat16):
    gain = levels(rng, dims, cuts, -0.22, 0.18) if cuts else 1.0
    array = jax.random.normal(rng, dims, jnp.float32) * width * gain
    return jnp.minimum(jnp.maximum(array, -bound), bound).astype(held_as)


def setup_inputs(seed: int = 0, part: int = 0) -> dict:
    splits = jax.random.split(jax.random.key(seed), 10)
    own_keys = jax.random.split(jax.random.fold_in(splits[9], part), 10)
    tokens = noise(own_keys[0], (TOKENS, D), 1.0, 6.0, ((0, 16),))
    pseudo = noise(own_keys[1], (TOKENS, TOPK, FF), 1.0, 6.0, ((0, 16),))
    assign_keys = jax.random.split(jax.random.fold_in(own_keys[2], 1), TOKENS // TOK_DEV)
    assign_turns = jax.random.permutation(jax.random.fold_in(own_keys[2], 3), TOKENS // TOK_DEV)
    assign = jax.vmap(lambda own, number: deal_out(jax.random.fold_in(own_keys[2], 2), own, number, TOK_DEV, ROUTED, TOPK, CAP, 2))(assign_keys, assign_turns).reshape((TOKENS, TOPK))
    counts = with_ends(jax.random.randint(own_keys[3], (EXPERTS,), TOKENS * TOPK // (2 * ROUTED), 2 * TOKENS * TOPK // ROUTED + 1), jax.random.fold_in(own_keys[3], 1), TOKENS * TOPK // (2 * ROUTED), (2 * TOKENS * TOPK // ROUTED + 1) - 1).astype(jnp.int32)
    basis_act = noise(own_keys[4], (EXPERTS, D, EIG), D ** -0.5, 0.09375, ((0, 4), (1, 2), (2, 2)))
    basis_grad = noise(own_keys[5], (EXPERTS, FF, FF), FF ** -0.5, 0.15625, ((0, 4), (1, 2), (2, 2)))
    queries_act = noise(own_keys[6], (NQ, D), 1.0, 6.0, ((1, 2),))
    queries_grad = noise(own_keys[7], (NQ, FF), 1.0, 6.0, ((1, 2),))
    query_expert_keys = jax.random.split(jax.random.fold_in(own_keys[8], 1), NQ // NQ)
    query_expert_turns = jax.random.permutation(jax.random.fold_in(own_keys[8], 3), NQ // NQ)
    query_expert = jax.vmap(lambda own, number: deal_out(jax.random.fold_in(own_keys[8], 2), own, number, NQ, EXPERTS, 1, QCAP, 2))(query_expert_keys, query_expert_turns).reshape((NQ, 1))
    return dict(tokens=tokens, pseudo=pseudo, assign=assign, counts=counts, basis_act=basis_act, basis_grad=basis_grad, queries_act=queries_act, queries_grad=queries_grad, query_expert=query_expert)


def reference(tokens, pseudo, assign, counts, basis_act, basis_grad, queries_act, queries_grad, query_expert):
    row_span = (TOKENS // TOK_DEV) * CAP

    def factor_pair(expert_id):
        routed = (assign == expert_id).astype(jnp.int32)
        token_used = jnp.sum(routed, axis=1)
        row_order = jnp.argsort(1 - token_used, stable=True)[:row_span].astype(jnp.int32)
        row_weight = token_used[row_order].astype(jnp.float32)
        act_rows = tokens[row_order].astype(jnp.float32) * row_weight[:, None]
        slot_hits = routed[row_order].astype(jnp.float32)
        grad_rows = jnp.sum(pseudo[row_order].astype(jnp.float32) * slot_hits[:, :, None], axis=1)
        act_sum = jnp.dot(act_rows.T, act_rows, preferred_element_type=jnp.float32)
        grad_sum = jnp.dot(grad_rows.T, grad_rows, preferred_element_type=jnp.float32)
        inverse = 1.0 / counts[expert_id].astype(jnp.float32)
        return (act_sum * inverse).astype(jnp.bfloat16), (grad_sum * inverse).astype(jnp.bfloat16)

    act_cov, grad_cov = lax.map(factor_pair, jnp.arange(EXPERTS, dtype=jnp.int32))

    query_ids = query_expert[:, 0]

    def visit_expert(totals, expert_id):
        act_acc, grad_acc = totals
        act_part = jnp.dot(queries_act, basis_act[expert_id], preferred_element_type=jnp.float32)
        grad_part = jnp.dot(queries_grad, basis_grad[expert_id], preferred_element_type=jnp.float32)
        is_mine = (query_ids == expert_id)[:, None]
        return (jnp.where(is_mine, act_part, act_acc), jnp.where(is_mine, grad_part, grad_acc)), None

    start_state = (jnp.zeros((query_ids.shape[0], basis_act.shape[2]), jnp.float32),
                   jnp.zeros((query_ids.shape[0], basis_grad.shape[2]), jnp.float32))
    (rot_act, rot_grad), _ = lax.scan(visit_expert, start_state, jnp.arange(EXPERTS, dtype=jnp.int32))
    return act_cov, grad_cov, rot_act.astype(jnp.bfloat16), rot_grad.astype(jnp.bfloat16)
```

```python
import functools

import jax
import jax.numpy as jnp
from jax import lax
from jax.experimental import pallas as pl
from jax.experimental.pallas import tpu as pltpu
from jax.sharding import PartitionSpec as P

CAP = 2
F32 = jnp.float32
BF16 = jnp.bfloat16
HBM = pl.BlockSpec(memory_space=pl.ANY)
VMEM = pl.BlockSpec(memory_space=pltpu.VMEM)
SMEM = pl.BlockSpec(memory_space=pltpu.SMEM)


def partner_order(experts, blocks):
    away = [(de, dd) for dd in range(blocks) for de in range(experts - 1, 0, -1)]
    away += [(0, dd) for dd in range(1, blocks)] + [(0, 0)]
    half = experts * blocks // 2
    near = [p for p in away if p[1] == 0 and p[0] > 0] + [p for p in away if p[0] == 0 and p[1] > 0]
    far = [p for p in away if p not in near and p != (0, 0)] + [(0, 0)]
    order = (near + far)[:half], (near + far)[half:]
    return order


def dot(a, b):
    return jnp.dot(a, b, preferred_element_type=F32)


def by_row(table, rows, per):
    index = lax.broadcasted_iota(jnp.int32, (rows, 1), 0) // per
    value = jnp.zeros((rows, 1), jnp.int32)
    for i, entry in enumerate(table):
        if entry:
            value = jnp.where(index == i, entry, value)
    return value


def pack_kernel(
    order,
    row_out,
    assign_hbm,
    tokens_hbm,
    pseudo_hbm,
    qe_hbm,
    qa_hbm,
    qg_hbm,
    ba_hbm,
    bg_hbm,
    keep_ref,
    give_ref,
    assign_ref,
    tokens_ref,
    pseudo_ref,
    qe_ref,
    qa_ref,
    qg_ref,
    ba_ref,
    bg_ref,
    sems,
):
    chunks = 4
    deep = ba_ref.shape[0] // chunks
    small = [
        pltpu.make_async_copy(src, dst, sems.at[i])
        for i, (src, dst) in enumerate(
            [
                (assign_hbm, assign_ref),
                (qe_hbm, qe_ref),
                (qa_hbm, qa_ref),
                (qg_hbm, qg_ref),
                (tokens_hbm, tokens_ref),
                (pseudo_hbm, pseudo_ref),
                (bg_hbm, bg_ref),
            ]
        )
    ]
    large = [
        pltpu.make_async_copy(
            ba_hbm.at[pl.ds(i * deep, deep)], ba_ref.at[pl.ds(i * deep, deep)], sems.at[len(small) + i]
        )
        for i in range(chunks)
    ]
    for copy in small + large:
        copy.start()
    expert, block, core = lax.axis_index("expert"), lax.axis_index("dp"), lax.axis_index("mp")
    half = len(order[0])
    rows = 4 * half
    blocks = 1 + max(dd for _, dd in order[0] + order[1])
    slots, toks = assign_ref.shape
    flat = slots * toks
    d_model, hidden = tokens_ref.shape[1], pseudo_ref.shape[1]
    plan = [order[0] + order[1], order[1] + order[0]]
    step_e = jnp.where(core == 0, by_row([p[0] for p in plan[0]], rows, 2), by_row([p[0] for p in plan[1]], rows, 2))
    step_d = jnp.where(core == 0, by_row([p[1] for p in plan[0]], rows, 2), by_row([p[1] for p in plan[1]], rows, 2))
    to_e, to_d = step_e ^ expert, step_d ^ block
    second = lax.broadcasted_iota(jnp.int32, (rows, 1), 0) % 2

    small[0].wait()
    spread = (
        lax.broadcasted_iota(jnp.int32, (toks, flat), 0)
        == lax.broadcasted_iota(jnp.int32, (toks, flat), 1) // slots
    ).astype(F32)
    ids = dot(assign_ref[...].astype(F32), spread)
    mine = (
        lax.broadcasted_iota(jnp.int32, (slots, flat), 0)
        == lax.broadcasted_iota(jnp.int32, (slots, flat), 1) % slots
    )
    ids = jnp.sum(jnp.where(mine, ids, 0.0), axis=0, keepdims=True).astype(jnp.int32)
    place = lax.broadcasted_iota(jnp.int32, (rows, flat), 1)
    hit = ids == to_e
    first = jnp.min(jnp.where(hit, place, flat), axis=1, keepdims=True)
    last = jnp.max(jnp.where(hit, place, -1), axis=1, keepdims=True)
    chosen = jnp.where(second == 0, first, jnp.where(last == first, -1, last))
    slot_pick = (place == chosen).astype(BF16)
    low = lax.broadcasted_iota(jnp.int32, (rows, toks), 1) * slots
    token_pick = ((chosen >= low) & (chosen < low + slots)).astype(BF16)

    def put(column, value):
        value = value.astype(BF16)
        width = value.shape[1]
        for i in range(half):
            keep_ref[i, :, column : column + width] = value[2 * i : 2 * i + 2]
            give_ref[i, :, column : column + width] = value[2 * (half + i) : 2 * (half + i) + 2]

    small[4].wait()
    put(0, dot(token_pick, tokens_ref[...]))
    small[5].wait()
    put(d_model, dot(slot_pick, pseudo_ref[...]))

    for i in (1, 2, 3):
        small[i].wait()
    queries = qa_ref.shape[0]
    base = d_model + hidden
    act_cols, grad_cols = ba_ref.shape[1], bg_ref.shape[1]
    asked = qe_ref[...] == expert
    query = lax.broadcasted_iota(jnp.int32, (rows, queries), 1)
    picks = []
    for i in range(row_out // 2):
        picks.append(
            ((query == (to_e * blocks + to_d) * row_out + 2 * i + second) & asked).astype(BF16)
        )
    pick = jnp.concatenate(picks, axis=0) if len(picks) > 1 else picks[0]
    my_act = dot(pick, qa_ref[...]).astype(BF16)
    my_grad = dot(pick, qg_ref[...]).astype(BF16)
    small[6].wait()
    grad_part = dot(my_grad, bg_ref[...])
    act_part = jnp.zeros((my_act.shape[0], act_cols), F32)
    for c in range(chunks):
        large[c].wait()
        act_part += dot(my_act[:, c * deep : (c + 1) * deep], ba_ref[c * deep : (c + 1) * deep])
    act_high = act_part.astype(BF16)
    grad_high = grad_part.astype(BF16)
    act_low = act_part - act_high.astype(F32)
    grad_low = grad_part - grad_high.astype(F32)
    width = 2 * (act_cols + grad_cols)
    for i in range(row_out // 2):
        cut = slice(i * rows, (i + 1) * rows)
        at = base + i * width
        put(at, act_high[cut])
        put(at + act_cols, grad_high[cut])
        put(at + act_cols + grad_cols, act_low[cut])
        put(at + 2 * act_cols + grad_cols, grad_low[cut])


def pack(order, row_out, assign, tokens, pseudo, qe, qa, qg, ba, bg):
    width = tokens.shape[1] + pseudo.shape[1] + row_out * (ba.shape[1] + bg.shape[1])
    out = jax.ShapeDtypeStruct((len(order[0]), CAP, width), BF16)
    operands = (assign, tokens, pseudo, qe, qa, qg, ba, bg)
    return pl.pallas_call(
        functools.partial(pack_kernel, order, row_out),
        out_shape=(out, out),
        in_specs=[HBM] * len(operands),
        out_specs=(VMEM, VMEM),
        scratch_shapes=[pltpu.VMEM(x.shape, x.dtype) for x in operands]
        + [pltpu.SemaphoreType.DMA((11,))],
        compiler_params=pltpu.CompilerParams(vmem_limit_bytes=32 * 1024 * 1024),
        name="select_rows_and_rotate_queries",
    )(*operands)


def factor_kernel(
    act_width,
    row_out,
    act_cols,
    count_ref,
    here_ref,
    there_ref,
    act_hbm,
    grad_hbm,
    rot_act_ref,
    rot_grad_ref,
    rows_ref,
    act_ref,
    grad_ref,
    sems,
):
    block, core = lax.axis_index("dp"), lax.axis_index("mp")
    half = here_ref.shape[0]
    act_block, act_half = act_ref.shape
    grad_block, grad_half = grad_ref.shape
    wide = act_width + 2 * grad_half
    inverse = 1.0 / count_ref[0].astype(F32)
    pieces = []
    for ref in (here_ref, there_ref):
        for i in range(half):
            for c in range(2):
                pieces.append(ref[i, c, :, :wide])
    rows_ref[...] = jnp.concatenate(pieces, axis=0)

    contract = (((0,), (0,)), ((), ()))
    grad_left = rows_ref[:, pl.ds(pl.multiple_of(act_width + block * grad_block, 128), grad_block)]
    grad_right = rows_ref[:, pl.ds(pl.multiple_of(act_width + core * grad_half, 128), grad_half)]
    grad_sum = lax.dot_general(grad_left, grad_right, contract, preferred_element_type=F32)
    grad_ref[...] = (grad_sum * inverse).astype(BF16)
    grad_copy = pltpu.make_async_copy(grad_ref, grad_hbm, sems.at[0])
    grad_copy.start()

    step = 256
    count = act_block // step
    right = rows_ref[:, pl.ds(pl.multiple_of(core * act_half, 128), act_half)]
    copies = []
    for i in range(count):
        at = pl.multiple_of(block * act_block + i * step, 128)
        left = rows_ref[:, pl.ds(at, step)]
        part = lax.dot_general(left, right, contract, preferred_element_type=F32)
        act_ref[i * step : (i + 1) * step, :] = (part * inverse).astype(BF16)
        copy = pltpu.make_async_copy(
            act_ref.at[pl.ds(i * step, step)], act_hbm.at[pl.ds(i * step, step)], sems.at[1 + i]
        )
        copy.start()
        copies.append(copy)

    cols = act_cols + rot_grad_ref.shape[1]
    for i in range(row_out // 2):
        at = wide + i * 2 * cols
        total = jnp.zeros((2, cols), F32)
        for ref, c in ((here_ref, 0), (there_ref, 1)):
            for r in range(half):
                high = ref[r, c, :, at : at + cols].astype(F32)
                low = ref[r, c, :, at + cols : at + 2 * cols].astype(F32)
                total += high + low
        rot_act_ref[2 * i : 2 * i + 2, :] = total[:, :act_cols].astype(BF16)
        rot_grad_ref[2 * i : 2 * i + 2, :] = total[:, act_cols:].astype(BF16)
    grad_copy.wait()
    for copy in copies:
        copy.wait()


def factors(act_width, row_out, act_tile, grad_tile, act_cols, grad_cols, counts, here, there):
    rows = 2 * here.shape[0] * here.shape[1] * here.shape[2]
    wide = act_width + 2 * grad_tile[1]
    return pl.pallas_call(
        functools.partial(factor_kernel, act_width, row_out, act_cols),
        out_shape=(
            jax.ShapeDtypeStruct(act_tile, BF16),
            jax.ShapeDtypeStruct(grad_tile, BF16),
            jax.ShapeDtypeStruct((row_out, act_cols), BF16),
            jax.ShapeDtypeStruct((row_out, grad_cols), BF16),
        ),
        in_specs=[SMEM, VMEM, VMEM],
        out_specs=(HBM, HBM, VMEM, VMEM),
        scratch_shapes=[
            pltpu.VMEM((rows, wide), BF16),
            pltpu.VMEM(act_tile, BF16),
            pltpu.VMEM(grad_tile, BF16),
            pltpu.SemaphoreType.DMA((1 + act_tile[0] // 256,)),
        ],
        compiler_params=pltpu.CompilerParams(vmem_limit_bytes=40 * 1024 * 1024),
        name="factor_tiles",
    )(counts, here, there)


def local(
    tokens, pseudo, assign, counts, basis_act, basis_grad, queries_act, queries_grad, query_expert
):
    experts, blocks = lax.axis_size("expert"), lax.axis_size("dp")
    toks, d_model = tokens.shape
    slots, hidden = pseudo.shape[1], pseudo.shape[2]
    row_out = query_expert.shape[0] // (experts * blocks)
    order = partner_order(experts, blocks)
    half = len(order[0])
    keep, give = pack(
        order,
        row_out,
        assign.T,
        tokens,
        pseudo.reshape(toks * slots, hidden),
        query_expert.T,
        queries_act,
        queries_grad,
        basis_act[0],
        basis_grad[0],
    )
    swap = [(0, 1), (1, 0)]
    got = lax.ppermute(give, "mp", swap)
    arrived = []
    for r in range(half):
        pairs = [
            ((e * blocks + d) * 2 + m, ((e ^ order[m][r][0]) * blocks + (d ^ order[m][r][1])) * 2 + m)
            for e in range(experts)
            for d in range(blocks)
            for m in range(2)
        ]
        arrived.append(lax.ppermute(jnp.stack([keep[r], got[r]]), ("expert", "dp", "mp"), pairs))
    here = jnp.stack(arrived)
    there = lax.ppermute(here, "mp", swap)
    act_cov, grad_cov, rot_act, rot_grad = factors(
        d_model,
        row_out,
        (d_model // blocks, d_model // 2),
        (hidden // blocks, hidden // 2),
        basis_act.shape[2],
        basis_grad.shape[2],
        counts,
        here,
        there,
    )
    return act_cov[None], grad_cov[None], rot_act, rot_grad


def solution(mesh):
    return jax.shard_map(
        local,
        mesh=mesh,
        in_specs=(
            P(("groups", "expert", "dp", "mp"), None),
            P(("groups", "expert", "dp", "mp"), None, None),
            P(("groups", "expert", "dp", "mp"), None),
            P(("groups", "expert")),
            P(("groups", "expert"), "dp", "mp"),
            P(("groups", "expert"), "dp", "mp"),
            P("groups", "dp"),
            P("groups", "dp"),
            P("groups", None),
        ),
        out_specs=(
            P(("groups", "expert"), "dp", "mp"),
            P(("groups", "expert"), "dp", "mp"),
            P(("groups", "expert", "dp"), "mp"),
            P(("groups", "expert", "dp"), "mp"),
        ),
        check_vma=False,
    )
```

```python
import functools

import jax
import jax.numpy as jnp
from jax import lax
from jax.experimental import pallas as pl
from jax.experimental.pallas import tpu as pltpu
from jax.sharding import PartitionSpec as P

CAP = 2
F32 = jnp.float32
BF16 = jnp.bfloat16
HBM = pl.BlockSpec(memory_space=pltpu.HBM)
VMEM = pl.BlockSpec(memory_space=pltpu.VMEM)
SMEM = pl.BlockSpec(memory_space=pltpu.SMEM)


def partner_order(experts, blocks):
    away = [(de, dd) for dd in range(blocks) for de in range(experts - 1, 0, -1)]
    away += [(0, dd) for dd in range(1, blocks)] + [(0, 0)]
    half = experts * blocks // 2
    near = [p for p in away if p[1] == 0 and p[0] > 0] + [p for p in away if p[0] == 0 and p[1] > 0]
    far = [p for p in away if p not in near and p != (0, 0)] + [(0, 0)]
    order = (near + far)[:half], (near + far)[half:]
    return order


def dot(a, b):
    return jnp.dot(a, b, preferred_element_type=F32)


def by_row(table, rows, per):
    index = lax.broadcasted_iota(jnp.int32, (rows, 1), 0) // per
    value = jnp.zeros((rows, 1), jnp.int32)
    for i, entry in enumerate(table):
        if entry:
            value = jnp.where(index == i, entry, value)
    return value


def pack_kernel(
    order,
    row_out,
    assign_hbm,
    tokens_hbm,
    pseudo_hbm,
    qe_hbm,
    qa_hbm,
    qg_hbm,
    ba_hbm,
    bg_hbm,
    keep_ref,
    give_ref,
    assign_ref,
    tokens_ref,
    pseudo_ref,
    qe_ref,
    qa_ref,
    qg_ref,
    ba_ref,
    bg_ref,
    sems,
):
    chunks = 4
    deep = ba_ref.shape[0] // chunks
    small = [
        pltpu.make_async_copy(src, dst, sems.at[i])
        for i, (src, dst) in enumerate(
            [
                (assign_hbm, assign_ref),
                (qe_hbm, qe_ref),
                (qa_hbm, qa_ref),
                (qg_hbm, qg_ref),
                (tokens_hbm, tokens_ref),
                (pseudo_hbm, pseudo_ref),
                (bg_hbm, bg_ref),
            ]
        )
    ]
    large = [
        pltpu.make_async_copy(
            ba_hbm.at[pl.ds(i * deep, deep)], ba_ref.at[pl.ds(i * deep, deep)], sems.at[len(small) + i]
        )
        for i in range(chunks)
    ]
    for copy in small + large:
        copy.start()
    expert, block, core = lax.axis_index("expert"), lax.axis_index("dp"), lax.axis_index("mp")
    half = len(order[0])
    rows = 4 * half
    blocks = 1 + max(dd for _, dd in order[0] + order[1])
    slots, toks = assign_ref.shape
    flat = slots * toks
    d_model, hidden = tokens_ref.shape[1], pseudo_ref.shape[1]
    plan = [order[0] + order[1], order[1] + order[0]]
    step_e = jnp.where(core == 0, by_row([p[0] for p in plan[0]], rows, 2), by_row([p[0] for p in plan[1]], rows, 2))
    step_d = jnp.where(core == 0, by_row([p[1] for p in plan[0]], rows, 2), by_row([p[1] for p in plan[1]], rows, 2))
    to_e, to_d = step_e ^ expert, step_d ^ block
    second = lax.broadcasted_iota(jnp.int32, (rows, 1), 0) % 2

    small[0].wait()
    spread = (
        lax.broadcasted_iota(jnp.int32, (toks, flat), 0)
        == lax.broadcasted_iota(jnp.int32, (toks, flat), 1) // slots
    ).astype(F32)
    ids = dot(assign_ref[...].astype(F32), spread)
    mine = (
        lax.broadcasted_iota(jnp.int32, (slots, flat), 0)
        == lax.broadcasted_iota(jnp.int32, (slots, flat), 1) % slots
    )
    ids = jnp.sum(jnp.where(mine, ids, 0.0), axis=0, keepdims=True).astype(jnp.int32)
    place = lax.broadcasted_iota(jnp.int32, (rows, flat), 1)
    hit = ids == to_e
    first = jnp.min(jnp.where(hit, place, flat), axis=1, keepdims=True)
    last = jnp.max(jnp.where(hit, place, -1), axis=1, keepdims=True)
    chosen = jnp.where(second == 0, first, jnp.where(last == first, -1, last))
    slot_pick = (place == chosen).astype(BF16)
    low = lax.broadcasted_iota(jnp.int32, (rows, toks), 1) * slots
    token_pick = ((chosen >= low) & (chosen < low + slots)).astype(BF16)

    def put(column, value):
        value = value.astype(BF16)
        width = value.shape[1]
        for i in range(half):
            keep_ref[i, :, column : column + width] = value[2 * i : 2 * i + 2]
            give_ref[i, :, column : column + width] = value[2 * (half + i) : 2 * (half + i) + 2]

    small[4].wait()
    put(0, dot(token_pick, tokens_ref[...]))
    small[5].wait()
    put(d_model, dot(slot_pick, pseudo_ref[...]))

    for i in (1, 2, 3):
        small[i].wait()
    queries = qa_ref.shape[0]
    base = d_model + hidden
    act_cols, grad_cols = ba_ref.shape[1], bg_ref.shape[1]
    asked = qe_ref[...] == expert
    query = lax.broadcasted_iota(jnp.int32, (rows, queries), 1)
    picks = []
    for i in range(row_out // 2):
        picks.append(
            ((query == (to_e * blocks + to_d) * row_out + 2 * i + second) & asked).astype(BF16)
        )
    pick = jnp.concatenate(picks, axis=0) if len(picks) > 1 else picks[0]
    my_act = dot(pick, qa_ref[...]).astype(BF16)
    my_grad = dot(pick, qg_ref[...]).astype(BF16)
    small[6].wait()
    grad_part = dot(my_grad, bg_ref[...])
    act_part = jnp.zeros((my_act.shape[0], act_cols), F32)
    for c in range(chunks):
        large[c].wait()
        act_part += dot(my_act[:, c * deep : (c + 1) * deep], ba_ref[c * deep : (c + 1) * deep])
    act_high = act_part.astype(BF16)
    grad_high = grad_part.astype(BF16)
    act_low = act_part - act_high.astype(F32)
    grad_low = grad_part - grad_high.astype(F32)
    width = 2 * (act_cols + grad_cols)
    for i in range(row_out // 2):
        cut = slice(i * rows, (i + 1) * rows)
        at = base + i * width
        put(at, act_high[cut])
        put(at + act_cols, grad_high[cut])
        put(at + act_cols + grad_cols, act_low[cut])
        put(at + 2 * act_cols + grad_cols, grad_low[cut])


def pack(order, row_out, assign, tokens, pseudo, qe, qa, qg, ba, bg):
    width = tokens.shape[1] + pseudo.shape[1] + row_out * (ba.shape[1] + bg.shape[1])
    out = jax.ShapeDtypeStruct((len(order[0]), CAP, width), BF16)
    operands = (assign, tokens, pseudo, qe, qa, qg, ba, bg)
    operands = tuple(pltpu.with_memory_space_constraint(x, pltpu.HBM) for x in operands)
    return pl.pallas_call(
        functools.partial(pack_kernel, order, row_out),
        out_shape=(out, out),
        in_specs=[HBM] * len(operands),
        out_specs=(VMEM, VMEM),
        scratch_shapes=[pltpu.VMEM(x.shape, x.dtype) for x in operands]
        + [pltpu.SemaphoreType.DMA((11,))],
        compiler_params=pltpu.CompilerParams(vmem_limit_bytes=32 * 1024 * 1024),
        name="select_rows_and_rotate_queries",
    )(*operands)


def factor_kernel(
    act_width,
    row_out,
    act_cols,
    count_ref,
    here_ref,
    there_ref,
    act_hbm,
    grad_hbm,
    rot_act_ref,
    rot_grad_ref,
    rows_ref,
    act_ref,
    grad_ref,
    sems,
):
    block, core = lax.axis_index("dp"), lax.axis_index("mp")
    half = here_ref.shape[0]
    act_block, act_half = act_ref.shape
    grad_block, grad_half = grad_ref.shape
    wide = act_width + 2 * grad_half
    inverse = 1.0 / count_ref[0].astype(F32)
    pieces = []
    for ref in (here_ref, there_ref):
        for i in range(half):
            for c in range(2):
                pieces.append(ref[i, c, :, :wide])
    rows_ref[...] = jnp.concatenate(pieces, axis=0)

    contract = (((0,), (0,)), ((), ()))
    grad_left = rows_ref[:, pl.ds(pl.multiple_of(act_width + block * grad_block, 128), grad_block)]
    grad_right = rows_ref[:, pl.ds(pl.multiple_of(act_width + core * grad_half, 128), grad_half)]
    grad_sum = lax.dot_general(grad_left, grad_right, contract, preferred_element_type=F32)
    grad_ref[...] = (grad_sum * inverse).astype(BF16)
    grad_copy = pltpu.make_async_copy(grad_ref, grad_hbm, sems.at[0])
    grad_copy.start()

    step = 256
    count = act_block // step
    right = rows_ref[:, pl.ds(pl.multiple_of(core * act_half, 128), act_half)]
    copies = []
    for i in range(count):
        at = pl.multiple_of(block * act_block + i * step, 128)
        left = rows_ref[:, pl.ds(at, step)]
        part = lax.dot_general(left, right, contract, preferred_element_type=F32)
        act_ref[i * step : (i + 1) * step, :] = (part * inverse).astype(BF16)
        copy = pltpu.make_async_copy(
            act_ref.at[pl.ds(i * step, step)], act_hbm.at[pl.ds(i * step, step)], sems.at[1 + i]
        )
        copy.start()
        copies.append(copy)

    cols = act_cols + rot_grad_ref.shape[1]
    for i in range(row_out // 2):
        at = wide + i * 2 * cols
        total = jnp.zeros((2, cols), F32)
        for ref, c in ((here_ref, 0), (there_ref, 1)):
            for r in range(half):
                high = ref[r, c, :, at : at + cols].astype(F32)
                low = ref[r, c, :, at + cols : at + 2 * cols].astype(F32)
                total += high + low
        rot_act_ref[2 * i : 2 * i + 2, :] = total[:, :act_cols].astype(BF16)
        rot_grad_ref[2 * i : 2 * i + 2, :] = total[:, act_cols:].astype(BF16)
    grad_copy.wait()
    for copy in copies:
        copy.wait()


def factors(act_width, row_out, act_tile, grad_tile, act_cols, grad_cols, counts, here, there):
    rows = 2 * here.shape[0] * here.shape[1] * here.shape[2]
    wide = act_width + 2 * grad_tile[1]
    return pl.pallas_call(
        functools.partial(factor_kernel, act_width, row_out, act_cols),
        out_shape=(
            jax.ShapeDtypeStruct(act_tile, BF16),
            jax.ShapeDtypeStruct(grad_tile, BF16),
            jax.ShapeDtypeStruct((row_out, act_cols), BF16),
            jax.ShapeDtypeStruct((row_out, grad_cols), BF16),
        ),
        in_specs=[SMEM, VMEM, VMEM],
        out_specs=(HBM, HBM, VMEM, VMEM),
        scratch_shapes=[
            pltpu.VMEM((rows, wide), BF16),
            pltpu.VMEM(act_tile, BF16),
            pltpu.VMEM(grad_tile, BF16),
            pltpu.SemaphoreType.DMA((1 + act_tile[0] // 256,)),
        ],
        compiler_params=pltpu.CompilerParams(vmem_limit_bytes=40 * 1024 * 1024),
        name="factor_tiles",
    )(counts, here, there)


def local(
    tokens, pseudo, assign, counts, basis_act, basis_grad, queries_act, queries_grad, query_expert
):
    experts, blocks = lax.axis_size("expert"), lax.axis_size("dp")
    toks, d_model = tokens.shape
    slots, hidden = pseudo.shape[1], pseudo.shape[2]
    row_out = query_expert.shape[0] // (experts * blocks)
    order = partner_order(experts, blocks)
    half = len(order[0])
    keep, give = pack(
        order,
        row_out,
        assign.T,
        tokens,
        pseudo.reshape(toks * slots, hidden),
        query_expert.T,
        queries_act,
        queries_grad,
        basis_act[0],
        basis_grad[0],
    )
    swap = [(0, 1), (1, 0)]
    got = lax.ppermute(give, "mp", swap)
    arrived = []
    for r in range(half):
        pairs = [
            ((e * blocks + d) * 2 + m, ((e ^ order[m][r][0]) * blocks + (d ^ order[m][r][1])) * 2 + m)
            for e in range(experts)
            for d in range(blocks)
            for m in range(2)
        ]
        arrived.append(lax.ppermute(jnp.stack([keep[r], got[r]]), ("expert", "dp", "mp"), pairs))
    here = jnp.stack(arrived)
    there = lax.ppermute(here, "mp", swap)
    act_cov, grad_cov, rot_act, rot_grad = factors(
        d_model,
        row_out,
        (d_model // blocks, d_model // 2),
        (hidden // blocks, hidden // 2),
        basis_act.shape[2],
        basis_grad.shape[2],
        counts,
        here,
        there,
    )
    return act_cov[None], grad_cov[None], rot_act, rot_grad


def solution(mesh):
    return jax.shard_map(
        local,
        mesh=mesh,
        in_specs=(
            P(("groups", "expert", "dp", "mp"), None),
            P(("groups", "expert", "dp", "mp"), None, None),
            P(("groups", "expert", "dp", "mp"), None),
            P(("groups", "expert")),
            P(("groups", "expert"), "dp", "mp"),
            P(("groups", "expert"), "dp", "mp"),
            P("groups", "dp"),
            P("groups", "dp"),
            P("groups", None),
        ),
        out_specs=(
            P(("groups", "expert"), "dp", "mp"),
            P(("groups", "expert"), "dp", "mp"),
            P(("groups", "expert", "dp"), "mp"),
            P(("groups", "expert", "dp"), "mp"),
        ),
        check_vma=False,
    )
```

```python
import functools

import jax
import jax.numpy as jnp
from jax import lax
from jax.experimental import pallas as pl
from jax.experimental.pallas import tpu as pltpu
from jax.sharding import PartitionSpec as P

CAP = 2
F32 = jnp.float32
BF16 = jnp.bfloat16
HBM = pl.BlockSpec(memory_space=pltpu.HBM)
VMEM = pl.BlockSpec(memory_space=pltpu.VMEM)
SMEM = pl.BlockSpec(memory_space=pltpu.SMEM)


def partner_order(experts, blocks):
    far = list(range(experts // 2, experts)) + list(range(experts // 2 - 1, 0, -1))
    order = [], []
    for de in far:
        for dd in range(blocks):
            order[dd % 2].append((de, dd))
    for i in range(blocks):
        order[i % 2].append((0, (i + 1) % blocks))
    return order


def dot(a, b):
    return jnp.dot(a, b, preferred_element_type=F32)


def by_row(table, rows, per):
    index = lax.broadcasted_iota(jnp.int32, (rows, 1), 0) // per
    value = jnp.zeros((rows, 1), jnp.int32)
    for i, entry in enumerate(table):
        if entry:
            value = jnp.where(index == i, entry, value)
    return value


def pack_kernel(
    order,
    row_out,
    assign_hbm,
    tokens_hbm,
    pseudo_hbm,
    qe_hbm,
    qa_hbm,
    qg_hbm,
    ba_hbm,
    bg_hbm,
    keep_ref,
    give_ref,
    assign_ref,
    tokens_ref,
    pseudo_ref,
    qe_ref,
    qa_ref,
    qg_ref,
    ba_ref,
    bg_ref,
    sems,
):
    chunks = 4
    deep = ba_ref.shape[0] // chunks
    small = [
        pltpu.make_async_copy(src, dst, sems.at[i])
        for i, (src, dst) in enumerate(
            [
                (assign_hbm, assign_ref),
                (qe_hbm, qe_ref),
                (qa_hbm, qa_ref),
                (qg_hbm, qg_ref),
                (tokens_hbm, tokens_ref),
                (pseudo_hbm, pseudo_ref),
                (bg_hbm, bg_ref),
            ]
        )
    ]
    large = [
        pltpu.make_async_copy(
            ba_hbm.at[pl.ds(i * deep, deep)], ba_ref.at[pl.ds(i * deep, deep)], sems.at[len(small) + i]
        )
        for i in range(chunks)
    ]
    for copy in small + large:
        copy.start()
    expert, block, core = lax.axis_index("expert"), lax.axis_index("dp"), lax.axis_index("mp")
    half = len(order[0])
    rows = 4 * half
    blocks = 1 + max(dd for _, dd in order[0] + order[1])
    slots, toks = assign_ref.shape
    flat = slots * toks
    d_model, hidden = tokens_ref.shape[1], pseudo_ref.shape[1]
    plan = [order[0] + order[1], order[1] + order[0]]
    step_e = jnp.where(core == 0, by_row([p[0] for p in plan[0]], rows, 2), by_row([p[0] for p in plan[1]], rows, 2))
    step_d = jnp.where(core == 0, by_row([p[1] for p in plan[0]], rows, 2), by_row([p[1] for p in plan[1]], rows, 2))
    to_e, to_d = step_e ^ expert, step_d ^ block
    second = lax.broadcasted_iota(jnp.int32, (rows, 1), 0) % 2

    small[0].wait()
    spread = (
        lax.broadcasted_iota(jnp.int32, (toks, flat), 0)
        == lax.broadcasted_iota(jnp.int32, (toks, flat), 1) // slots
    ).astype(F32)
    ids = dot(assign_ref[...].astype(F32), spread)
    mine = (
        lax.broadcasted_iota(jnp.int32, (slots, flat), 0)
        == lax.broadcasted_iota(jnp.int32, (slots, flat), 1) % slots
    )
    ids = jnp.sum(jnp.where(mine, ids, 0.0), axis=0, keepdims=True).astype(jnp.int32)
    place = lax.broadcasted_iota(jnp.int32, (rows, flat), 1)
    hit = ids == to_e
    first = jnp.min(jnp.where(hit, place, flat), axis=1, keepdims=True)
    last = jnp.max(jnp.where(hit, place, -1), axis=1, keepdims=True)
    chosen = jnp.where(second == 0, first, jnp.where(last == first, -1, last))
    slot_pick = (place == chosen).astype(BF16)
    low = lax.broadcasted_iota(jnp.int32, (rows, toks), 1) * slots
    token_pick = ((chosen >= low) & (chosen < low + slots)).astype(BF16)

    def put(column, value):
        value = value.astype(BF16)
        width = value.shape[1]
        for i in range(half):
            keep_ref[i, :, column : column + width] = value[2 * i : 2 * i + 2]
            give_ref[i, :, column : column + width] = value[2 * (half + i) : 2 * (half + i) + 2]

    small[4].wait()
    put(0, dot(token_pick, tokens_ref[...]))
    small[5].wait()
    put(d_model, dot(slot_pick, pseudo_ref[...]))

    for i in (1, 2, 3):
        small[i].wait()
    queries = qa_ref.shape[0]
    base = d_model + hidden
    act_cols, grad_cols = ba_ref.shape[1], bg_ref.shape[1]
    asked = qe_ref[...] == expert
    query = lax.broadcasted_iota(jnp.int32, (rows, queries), 1)
    picks = []
    for i in range(row_out // 2):
        picks.append(
            ((query == (to_e * blocks + to_d) * row_out + 2 * i + second) & asked).astype(BF16)
        )
    pick = jnp.concatenate(picks, axis=0) if len(picks) > 1 else picks[0]
    my_act = dot(pick, qa_ref[...]).astype(BF16)
    my_grad = dot(pick, qg_ref[...]).astype(BF16)
    small[6].wait()
    grad_part = dot(my_grad, bg_ref[...])
    act_part = jnp.zeros((my_act.shape[0], act_cols), F32)
    for c in range(chunks):
        large[c].wait()
        act_part += dot(my_act[:, c * deep : (c + 1) * deep], ba_ref[c * deep : (c + 1) * deep])
    act_high = act_part.astype(BF16)
    grad_high = grad_part.astype(BF16)
    act_low = act_part - act_high.astype(F32)
    grad_low = grad_part - grad_high.astype(F32)
    width = 2 * (act_cols + grad_cols)
    for i in range(row_out // 2):
        cut = slice(i * rows, (i + 1) * rows)
        at = base + i * width
        put(at, act_high[cut])
        put(at + act_cols, grad_high[cut])
        put(at + act_cols + grad_cols, act_low[cut])
        put(at + 2 * act_cols + grad_cols, grad_low[cut])


def pack(order, row_out, assign, tokens, pseudo, qe, qa, qg, ba, bg):
    width = tokens.shape[1] + pseudo.shape[1] + row_out * (ba.shape[1] + bg.shape[1])
    out = jax.ShapeDtypeStruct((len(order[0]), CAP, width), BF16)
    operands = (assign, tokens, pseudo, qe, qa, qg, ba, bg)
    operands = tuple(pltpu.with_memory_space_constraint(x, pltpu.HBM) for x in operands)
    return pl.pallas_call(
        functools.partial(pack_kernel, order, row_out),
        out_shape=(out, out),
        in_specs=[HBM] * len(operands),
        out_specs=(VMEM, VMEM),
        scratch_shapes=[pltpu.VMEM(x.shape, x.dtype) for x in operands]
        + [pltpu.SemaphoreType.DMA((11,))],
        compiler_params=pltpu.CompilerParams(vmem_limit_bytes=32 * 1024 * 1024),
        name="select_rows_and_rotate_queries",
    )(*operands)


def row_steps(rows):
    return [(i * 128, 64 if i < 2 else 128) for i in range(rows // 128)]


def factor_kernel(act_width, row_out, rounds, count_ref, *refs):
    here, there = refs[:rounds], refs[rounds : 2 * rounds]
    act_hbm, grad_hbm, rot_act_hbm, rot_grad_hbm = refs[2 * rounds : 2 * rounds + 4]
    right_ref, act_ref, grad_ref, rot_act_ref, rot_grad_ref, sems = refs[2 * rounds + 4 :]
    block, core = lax.axis_index("dp"), lax.axis_index("mp")
    act_block, act_half = act_ref.shape
    grad_block, grad_half = grad_ref.shape
    inverse = 1.0 / count_ref[0].astype(F32)
    contract = (((0,), (0,)), ((), ()))
    copies = []

    def send(src, dst):
        copy = pltpu.make_async_copy(src, dst, sems.at[len(copies)])
        copy.start()
        copies.append(copy)

    def columns(at, width):
        span = pl.ds(pl.multiple_of(at, 128), width)
        return jnp.concatenate([ref[c, :, span] for ref in here + there for c in range(2)], axis=0)

    def tile(left, right):
        part = lax.dot_general(left, right, contract, preferred_element_type=F32)
        return (part * inverse).astype(BF16)

    right_ref[...] = columns(core * act_half, act_half)
    for first, step in row_steps(act_block):
        left = columns(block * act_block + first, 128)
        for at in range(0, 128, step):
            rows = pl.ds(first + at, step)
            act_ref[rows, :] = tile(left[:, at : at + step], right_ref[...])
            send(act_ref.at[rows], act_hbm.at[rows])

    grad_ref[...] = tile(
        columns(act_width + block * grad_block, grad_block),
        columns(act_width + core * grad_half, grad_half),
    )
    send(grad_ref, grad_hbm)

    act_cols = rot_act_ref.shape[1]
    cols = act_cols + rot_grad_ref.shape[1]
    for i in range(row_out // 2):
        at = act_width + 2 * grad_half + i * 2 * cols
        total = jnp.zeros((2, cols), F32)
        for group, c in ((here, 0), (there, 1)):
            for ref in group:
                high = ref[c, :, at : at + cols].astype(F32)
                low = ref[c, :, at + cols : at + 2 * cols].astype(F32)
                total += high + low
        rot_act_ref[2 * i : 2 * i + 2, :] = total[:, :act_cols].astype(BF16)
        rot_grad_ref[2 * i : 2 * i + 2, :] = total[:, act_cols:].astype(BF16)
    send(rot_act_ref, rot_act_hbm)
    send(rot_grad_ref, rot_grad_hbm)
    for copy in copies:
        copy.wait()


def factors(act_width, row_out, act_tile, grad_tile, act_cols, grad_cols, counts, here, there):
    rounds = len(here)
    shapes = (act_tile, grad_tile, (row_out, act_cols), (row_out, grad_cols))
    return pl.pallas_call(
        functools.partial(factor_kernel, act_width, row_out, rounds),
        out_shape=tuple(jax.ShapeDtypeStruct(shape, BF16) for shape in shapes),
        in_specs=[SMEM] + [VMEM] * (2 * rounds),
        out_specs=(HBM,) * 4,
        scratch_shapes=[pltpu.VMEM((2 * 2 * CAP * rounds, act_tile[1]), BF16)]
        + [pltpu.VMEM(shape, BF16) for shape in shapes]
        + [pltpu.SemaphoreType.DMA((act_tile[0] // 128 + 5,))],
        compiler_params=pltpu.CompilerParams(vmem_limit_bytes=40 * 1024 * 1024),
        name="factor_tiles",
    )(counts, *here, *there)


def local(
    tokens, pseudo, assign, counts, basis_act, basis_grad, queries_act, queries_grad, query_expert
):
    experts, blocks = lax.axis_size("expert"), lax.axis_size("dp")
    toks, d_model = tokens.shape
    slots, hidden = pseudo.shape[1], pseudo.shape[2]
    row_out = query_expert.shape[0] // (experts * blocks)
    order = partner_order(experts, blocks)
    half = len(order[0])
    keep, give = pack(
        order,
        row_out,
        assign.T,
        tokens,
        pseudo.reshape(toks * slots, hidden),
        query_expert.T,
        queries_act,
        queries_grad,
        basis_act[0],
        basis_grad[0],
    )
    swap = [(0, 1), (1, 0)]
    got = lax.ppermute(give, "mp", swap)
    arrived = []
    for r in range(half):
        pairs = [
            ((e * blocks + d) * 2 + m, ((e ^ order[m][r][0]) * blocks + (d ^ order[m][r][1])) * 2 + m)
            for e in range(experts)
            for d in range(blocks)
            for m in range(2)
        ]
        arrived.append(lax.ppermute(jnp.stack([keep[r], got[r]]), ("expert", "dp", "mp"), pairs))
    there = [lax.ppermute(block, "mp", swap) for block in arrived]
    act_cov, grad_cov, rot_act, rot_grad = factors(
        d_model,
        row_out,
        (d_model // blocks, d_model // 2),
        (hidden // blocks, hidden // 2),
        basis_act.shape[2],
        basis_grad.shape[2],
        counts,
        arrived,
        there,
    )
    return act_cov[None], grad_cov[None], rot_act, rot_grad


def solution(mesh):
    return jax.shard_map(
        local,
        mesh=mesh,
        in_specs=(
            P(("groups", "expert", "dp", "mp"), None),
            P(("groups", "expert", "dp", "mp"), None, None),
            P(("groups", "expert", "dp", "mp"), None),
            P(("groups", "expert")),
            P(("groups", "expert"), "dp", "mp"),
            P(("groups", "expert"), "dp", "mp"),
            P("groups", "dp"),
            P("groups", "dp"),
            P("groups", None),
        ),
        out_specs=(
            P(("groups", "expert"), "dp", "mp"),
            P(("groups", "expert"), "dp", "mp"),
            P(("groups", "expert", "dp"), "mp"),
            P(("groups", "expert", "dp"), "mp"),
        ),
        check_vma=False,
    )
```

```python
import functools

import jax
import jax.numpy as jnp
from jax import lax
from jax.experimental import pallas as pl
from jax.experimental.pallas import tpu as pltpu
from jax.sharding import PartitionSpec as P

CAP = 2
CHUNKS = 8
F32 = jnp.float32
BF16 = jnp.bfloat16
HBM = pl.BlockSpec(memory_space=pltpu.HBM)
VMEM = pl.BlockSpec(memory_space=pltpu.VMEM)
SMEM = pl.BlockSpec(memory_space=pltpu.SMEM)


def partner_order(experts, blocks):
    far = list(range(experts // 2, experts)) + list(range(experts // 2 - 1, 0, -1))
    order = [], []
    for de in far:
        for dd in range(blocks):
            order[dd % 2].append((de, dd))
    for i in range(blocks):
        order[i % 2].append((0, (i + 1) % blocks))
    return order


def dot(a, b):
    return jnp.dot(a, b, preferred_element_type=F32)


def by_row(table, rows, per):
    index = lax.broadcasted_iota(jnp.int32, (rows, 1), 0) // per
    value = jnp.zeros((rows, 1), jnp.int32)
    for i, entry in enumerate(table):
        if entry:
            value = jnp.where(index == i, entry, value)
    return value


def pack_kernel(
    order,
    row_out,
    assign_hbm,
    tokens_hbm,
    pseudo_hbm,
    qe_hbm,
    qa_hbm,
    qg_hbm,
    ba_hbm,
    bg_hbm,
    *refs,
):
    half = len(order[0])
    send_refs, give_ref = refs[:half], refs[half]
    assign_ref, tokens_ref, pseudo_ref, qe_ref, qa_ref, qg_ref, ba_ref, bg_ref, sems = refs[half + 1 :]
    chunks = CHUNKS
    deep = ba_ref.shape[0] // chunks
    small = [
        pltpu.make_async_copy(src, dst, sems.at[i])
        for i, (src, dst) in enumerate(
            [
                (assign_hbm, assign_ref),
                (qe_hbm, qe_ref),
                (qa_hbm, qa_ref),
                (qg_hbm, qg_ref),
                (tokens_hbm, tokens_ref),
                (pseudo_hbm, pseudo_ref),
                (bg_hbm, bg_ref),
            ]
        )
    ]
    large = [
        pltpu.make_async_copy(
            ba_hbm.at[pl.ds(i * deep, deep)], ba_ref.at[pl.ds(i * deep, deep)], sems.at[len(small) + i]
        )
        for i in range(chunks)
    ]
    for copy in small + large:
        copy.start()
    expert, block, core = lax.axis_index("expert"), lax.axis_index("dp"), lax.axis_index("mp")
    rows = 4 * half
    blocks = 1 + max(dd for _, dd in order[0] + order[1])
    slots, toks = assign_ref.shape
    flat = slots * toks
    d_model, hidden = tokens_ref.shape[1], pseudo_ref.shape[1]
    plan = [order[0] + order[1], order[1] + order[0]]
    step_e = jnp.where(core == 0, by_row([p[0] for p in plan[0]], rows, 2), by_row([p[0] for p in plan[1]], rows, 2))
    step_d = jnp.where(core == 0, by_row([p[1] for p in plan[0]], rows, 2), by_row([p[1] for p in plan[1]], rows, 2))
    to_e, to_d = step_e ^ expert, step_d ^ block
    second = lax.broadcasted_iota(jnp.int32, (rows, 1), 0) % 2

    small[0].wait()
    spread = (
        lax.broadcasted_iota(jnp.int32, (toks, flat), 0)
        == lax.broadcasted_iota(jnp.int32, (toks, flat), 1) // slots
    ).astype(F32)
    ids = dot(assign_ref[...].astype(F32), spread)
    mine = (
        lax.broadcasted_iota(jnp.int32, (slots, flat), 0)
        == lax.broadcasted_iota(jnp.int32, (slots, flat), 1) % slots
    )
    ids = jnp.sum(jnp.where(mine, ids, 0.0), axis=0, keepdims=True).astype(jnp.int32)
    place = lax.broadcasted_iota(jnp.int32, (rows, flat), 1)
    hit = ids == to_e
    first = jnp.min(jnp.where(hit, place, flat), axis=1, keepdims=True)
    last = jnp.max(jnp.where(hit, place, -1), axis=1, keepdims=True)
    chosen = jnp.where(second == 0, first, jnp.where(last == first, -1, last))
    slot_pick = (place == chosen).astype(BF16)
    low = lax.broadcasted_iota(jnp.int32, (rows, toks), 1) * slots
    token_pick = ((chosen >= low) & (chosen < low + slots)).astype(BF16)

    def put(column, value):
        value = value.astype(BF16)
        width = value.shape[1]
        for i in range(half):
            send_refs[i][0, :, column : column + width] = value[2 * i : 2 * i + 2]
            give_ref[i, :, column : column + width] = value[2 * (half + i) : 2 * (half + i) + 2]

    small[4].wait()
    put(0, dot(token_pick, tokens_ref[...]))
    small[5].wait()
    put(d_model, dot(slot_pick, pseudo_ref[...]))

    for i in (1, 2, 3):
        small[i].wait()
    queries = qa_ref.shape[0]
    base = d_model + hidden
    act_cols, grad_cols = ba_ref.shape[1], bg_ref.shape[1]
    asked = qe_ref[...] == expert
    query = lax.broadcasted_iota(jnp.int32, (rows, queries), 1)
    picks = []
    for i in range(row_out // 2):
        picks.append(
            ((query == (to_e * blocks + to_d) * row_out + 2 * i + second) & asked).astype(BF16)
        )
    pick = jnp.concatenate(picks, axis=0) if len(picks) > 1 else picks[0]
    my_act = dot(pick, qa_ref[...]).astype(BF16)
    my_grad = dot(pick, qg_ref[...]).astype(BF16)
    width = 2 * (act_cols + grad_cols)

    def put_pair(column, value):
        high = value.astype(BF16)
        low = value - high.astype(F32)
        for i in range(row_out // 2):
            cut = slice(i * rows, (i + 1) * rows)
            put(base + i * width + column, high[cut])
            put(base + i * width + column + act_cols + grad_cols, low[cut])

    small[6].wait()
    put_pair(act_cols, dot(my_grad, bg_ref[...]))
    act_part = jnp.zeros((my_act.shape[0], act_cols), F32)
    for c in range(chunks):
        large[c].wait()
        act_part += dot(my_act[:, c * deep : (c + 1) * deep], ba_ref[c * deep : (c + 1) * deep])
    put_pair(0, act_part)


def pack(order, row_out, assign, tokens, pseudo, qe, qa, qg, ba, bg):
    width = tokens.shape[1] + pseudo.shape[1] + row_out * (ba.shape[1] + bg.shape[1])
    half = len(order[0])
    send = jax.ShapeDtypeStruct((2, CAP, width), BF16)
    give = jax.ShapeDtypeStruct((half, CAP, width), BF16)
    operands = (assign, tokens, pseudo, qe, qa, qg, ba, bg)
    operands = tuple(pltpu.with_memory_space_constraint(x, pltpu.HBM) for x in operands)
    return pl.pallas_call(
        functools.partial(pack_kernel, order, row_out),
        out_shape=(send,) * half + (give,),
        in_specs=[HBM] * len(operands),
        out_specs=(VMEM,) * (half + 1),
        scratch_shapes=[pltpu.VMEM(x.shape, x.dtype) for x in operands]
        + [pltpu.SemaphoreType.DMA((7 + CHUNKS,))],
        compiler_params=pltpu.CompilerParams(vmem_limit_bytes=32 * 1024 * 1024),
        name="select_rows_and_rotate_queries",
    )(*operands)


def row_steps(rows):
    return [(i * 128, 64 if i < 2 else 128) for i in range(rows // 128)]


def factor_kernel(act_width, row_out, rounds, count_ref, *refs):
    here, there = refs[:rounds], refs[rounds : 2 * rounds]
    act_hbm, grad_hbm, rot_act_hbm, rot_grad_hbm = refs[2 * rounds : 2 * rounds + 4]
    right_ref, act_ref, grad_ref, rot_act_ref, rot_grad_ref, sems = refs[2 * rounds + 4 :]
    block, core = lax.axis_index("dp"), lax.axis_index("mp")
    act_block, act_half = act_ref.shape
    grad_block, grad_half = grad_ref.shape
    inverse = 1.0 / count_ref[0].astype(F32)
    contract = (((0,), (0,)), ((), ()))
    copies = []

    def send(src, dst):
        copy = pltpu.make_async_copy(src, dst, sems.at[len(copies)])
        copy.start()
        copies.append(copy)

    def columns(at, width):
        span = pl.ds(pl.multiple_of(at, 128), width)
        return jnp.concatenate([ref[c, :, span] for ref in here + there for c in range(2)], axis=0)

    def tile(left, right):
        part = lax.dot_general(left, right, contract, preferred_element_type=F32)
        return (part * inverse).astype(BF16)

    right_ref[...] = columns(core * act_half, act_half)
    for first, step in row_steps(act_block):
        left = columns(block * act_block + first, 128)
        for at in range(0, 128, step):
            rows = pl.ds(first + at, step)
            act_ref[rows, :] = tile(left[:, at : at + step], right_ref[...])
            send(act_ref.at[rows], act_hbm.at[rows])

    grad_ref[...] = tile(
        columns(act_width + block * grad_block, grad_block),
        columns(act_width + core * grad_half, grad_half),
    )
    send(grad_ref, grad_hbm)

    act_cols = rot_act_ref.shape[1]
    cols = act_cols + rot_grad_ref.shape[1]
    for i in range(row_out // 2):
        at = act_width + 2 * grad_half + i * 2 * cols
        total = jnp.zeros((2, cols), F32)
        for group, c in ((here, 0), (there, 1)):
            for ref in group:
                high = ref[c, :, at : at + cols].astype(F32)
                low = ref[c, :, at + cols : at + 2 * cols].astype(F32)
                total += high + low
        rot_act_ref[2 * i : 2 * i + 2, :] = total[:, :act_cols].astype(BF16)
        rot_grad_ref[2 * i : 2 * i + 2, :] = total[:, act_cols:].astype(BF16)
    send(rot_act_ref, rot_act_hbm)
    send(rot_grad_ref, rot_grad_hbm)
    for copy in copies:
        copy.wait()


def factors(act_width, row_out, act_tile, grad_tile, act_cols, grad_cols, counts, here, there):
    rounds = len(here)
    shapes = (act_tile, grad_tile, (row_out, act_cols), (row_out, grad_cols))
    return pl.pallas_call(
        functools.partial(factor_kernel, act_width, row_out, rounds),
        out_shape=tuple(jax.ShapeDtypeStruct(shape, BF16) for shape in shapes),
        in_specs=[SMEM] + [VMEM] * (2 * rounds),
        out_specs=(HBM,) * 4,
        scratch_shapes=[pltpu.VMEM((2 * 2 * CAP * rounds, act_tile[1]), BF16)]
        + [pltpu.VMEM(shape, BF16) for shape in shapes]
        + [pltpu.SemaphoreType.DMA((act_tile[0] // 128 + 5,))],
        compiler_params=pltpu.CompilerParams(vmem_limit_bytes=40 * 1024 * 1024),
        name="factor_tiles",
    )(counts, *here, *there)


def local(
    tokens, pseudo, assign, counts, basis_act, basis_grad, queries_act, queries_grad, query_expert
):
    experts, blocks = lax.axis_size("expert"), lax.axis_size("dp")
    toks, d_model = tokens.shape
    slots, hidden = pseudo.shape[1], pseudo.shape[2]
    row_out = query_expert.shape[0] // (experts * blocks)
    order = partner_order(experts, blocks)
    half = len(order[0])
    *sends, give = pack(
        order,
        row_out,
        assign.T,
        tokens,
        pseudo.reshape(toks * slots, hidden),
        query_expert.T,
        queries_act,
        queries_grad,
        basis_act[0],
        basis_grad[0],
    )
    swap = [(0, 1), (1, 0)]
    got = lax.ppermute(give, "mp", swap)
    arrived = []
    for r in reversed(range(half)):
        pairs = [
            ((e * blocks + d) * 2 + m, ((e ^ order[m][r][0]) * blocks + (d ^ order[m][r][1])) * 2 + m)
            for e in range(experts)
            for d in range(blocks)
            for m in range(2)
        ]
        merged = sends[r].at[1].set(got[r])
        arrived.append(lax.ppermute(merged, ("expert", "dp", "mp"), pairs))
    there = [lax.ppermute(block, "mp", swap) for block in arrived]
    act_cov, grad_cov, rot_act, rot_grad = factors(
        d_model,
        row_out,
        (d_model // blocks, d_model // 2),
        (hidden // blocks, hidden // 2),
        basis_act.shape[2],
        basis_grad.shape[2],
        counts,
        arrived,
        there,
    )
    return act_cov[None], grad_cov[None], rot_act, rot_grad


def solution(mesh):
    return jax.shard_map(
        local,
        mesh=mesh,
        in_specs=(
            P(("groups", "expert", "dp", "mp"), None),
            P(("groups", "expert", "dp", "mp"), None, None),
            P(("groups", "expert", "dp", "mp"), None),
            P(("groups", "expert")),
            P(("groups", "expert"), "dp", "mp"),
            P(("groups", "expert"), "dp", "mp"),
            P("groups", "dp"),
            P("groups", "dp"),
            P("groups", None),
        ),
        out_specs=(
            P(("groups", "expert"), "dp", "mp"),
            P(("groups", "expert"), "dp", "mp"),
            P(("groups", "expert", "dp"), "mp"),
            P(("groups", "expert", "dp"), "mp"),
        ),
        check_vma=False,
    )
```

```python
import functools

import jax
import jax.numpy as jnp
from jax import lax
from jax.experimental import pallas as pl
from jax.experimental.pallas import tpu as pltpu
from jax.sharding import PartitionSpec as P

CAP = 2
CHUNKS = 8
F32 = jnp.float32
BF16 = jnp.bfloat16
HBM = pl.BlockSpec(memory_space=pltpu.HBM)
VMEM = pl.BlockSpec(memory_space=pltpu.VMEM)
SMEM = pl.BlockSpec(memory_space=pltpu.SMEM)


def partner_order(experts, blocks):
    far = list(range(experts // 2, experts)) + list(range(experts // 2 - 1, 0, -1))
    return tuple([(de, dd) for de in far for dd in range(core, blocks, 2)] for core in range(2))


def dot(a, b):
    return jnp.dot(a, b, preferred_element_type=F32)


def by_row(table, rows, per):
    index = lax.broadcasted_iota(jnp.int32, (rows, 1), 0) // per
    value = jnp.zeros((rows, 1), jnp.int32)
    for i, entry in enumerate(table):
        if entry:
            value = jnp.where(index == i, entry, value)
    return value


def pack_kernel(order, blocks, row_out, *refs):
    assign_hbm, tokens_hbm, pseudo_hbm, qe_hbm, qa_hbm, qg_hbm, ba_hbm, bg_hbm = refs[:8]
    half = len(order[0])
    send_refs, near_refs, give_ref = refs[8 : 8 + half], refs[8 + half : 8 + half + blocks], refs[8 + half + blocks]
    assign_ref, tokens_ref, pseudo_ref, qe_ref, qa_ref, qg_ref, ba_ref, bg_ref, sems = refs[9 + half + blocks :]
    chunks = CHUNKS
    deep = ba_ref.shape[0] // chunks
    small = [
        pltpu.make_async_copy(src, dst, sems.at[i])
        for i, (src, dst) in enumerate(
            [
                (assign_hbm, assign_ref),
                (qe_hbm, qe_ref),
                (qa_hbm, qa_ref),
                (qg_hbm, qg_ref),
                (tokens_hbm, tokens_ref),
                (pseudo_hbm, pseudo_ref),
                (bg_hbm, bg_ref),
            ]
        )
    ]
    large = [
        pltpu.make_async_copy(
            ba_hbm.at[pl.ds(i * deep, deep)], ba_ref.at[pl.ds(i * deep, deep)], sems.at[len(small) + i]
        )
        for i in range(chunks)
    ]
    for copy in small + large:
        copy.start()
    expert, block, core = lax.axis_index("expert"), lax.axis_index("dp"), lax.axis_index("mp")
    rows = 2 * (2 * half + blocks)
    slots, toks = assign_ref.shape
    flat = slots * toks
    d_model, hidden = tokens_ref.shape[1], pseudo_ref.shape[1]
    same_expert = [(0, dd) for dd in range(blocks)]
    plan = [order[0] + order[1] + same_expert, order[1] + order[0] + same_expert]
    step_e = jnp.where(core == 0, by_row([p[0] for p in plan[0]], rows, 2), by_row([p[0] for p in plan[1]], rows, 2))
    step_d = jnp.where(core == 0, by_row([p[1] for p in plan[0]], rows, 2), by_row([p[1] for p in plan[1]], rows, 2))
    to_e, to_d = step_e ^ expert, step_d ^ block
    second = lax.broadcasted_iota(jnp.int32, (rows, 1), 0) % 2

    small[0].wait()
    spread = (
        lax.broadcasted_iota(jnp.int32, (toks, flat), 0)
        == lax.broadcasted_iota(jnp.int32, (toks, flat), 1) // slots
    ).astype(F32)
    ids = dot(assign_ref[...].astype(F32), spread)
    mine = (
        lax.broadcasted_iota(jnp.int32, (slots, flat), 0)
        == lax.broadcasted_iota(jnp.int32, (slots, flat), 1) % slots
    )
    ids = jnp.sum(jnp.where(mine, ids, 0.0), axis=0, keepdims=True).astype(jnp.int32)
    place = lax.broadcasted_iota(jnp.int32, (rows, flat), 1)
    hit = ids == to_e
    first = jnp.min(jnp.where(hit, place, flat), axis=1, keepdims=True)
    last = jnp.max(jnp.where(hit, place, -1), axis=1, keepdims=True)
    chosen = jnp.where(second == 0, first, jnp.where(last == first, -1, last))
    slot_pick = (place == chosen).astype(BF16)
    low = lax.broadcasted_iota(jnp.int32, (rows, toks), 1) * slots
    token_pick = ((chosen >= low) & (chosen < low + slots)).astype(BF16)

    def put(column, value):
        width = value.shape[1]
        for i in range(half):
            send_refs[i][0, :, column : column + width] = value[2 * i : 2 * i + 2]
            give_ref[i, :, column : column + width] = value[2 * (half + i) : 2 * (half + i) + 2]

    def put_rows(column, value):
        value = value.astype(BF16)
        put(column, value)
        width = value.shape[1]
        mine = value[4 * half : 4 * half + 2]
        give_ref[half, :, column : column + width] = mine
        for ref in near_refs:
            ref[0, :, column : column + width] = mine

    small[4].wait()
    put_rows(0, dot(token_pick, tokens_ref[...]))
    small[5].wait()
    put_rows(d_model, dot(slot_pick, pseudo_ref[...]))

    for i in (1, 2, 3):
        small[i].wait()
    queries = qa_ref.shape[0]
    base = d_model + hidden
    act_cols, grad_cols = ba_ref.shape[1], bg_ref.shape[1]
    asked = qe_ref[...] == expert
    query = lax.broadcasted_iota(jnp.int32, (rows, queries), 1)
    picks = []
    for i in range(row_out // 2):
        picks.append(
            ((query == (to_e * blocks + to_d) * row_out + 2 * i + second) & asked).astype(BF16)
        )
    pick = jnp.concatenate(picks, axis=0) if len(picks) > 1 else picks[0]
    my_act = dot(pick, qa_ref[...]).astype(BF16)
    my_grad = dot(pick, qg_ref[...]).astype(BF16)
    cols = act_cols + grad_cols

    def put_pair(column, value):
        high = value.astype(BF16)
        low = (value - high.astype(F32)).astype(BF16)
        width = value.shape[1]
        for i in range(row_out // 2):
            at = base + 2 * i * cols + column
            put(at, high[i * rows : (i + 1) * rows])
            put(at + cols, low[i * rows : (i + 1) * rows])
            at = base + i * cols + column
            for dd, ref in enumerate(near_refs):
                first = i * rows + 4 * half + 2 * dd
                ref[0, :, at : at + width] = high[first : first + 2]
                ref[1, :, at : at + width] = low[first : first + 2]

    small[6].wait()
    put_pair(act_cols, dot(my_grad, bg_ref[...]))
    act_part = jnp.zeros((my_act.shape[0], act_cols), F32)
    for c in range(chunks):
        large[c].wait()
        act_part += dot(my_act[:, c * deep : (c + 1) * deep], ba_ref[c * deep : (c + 1) * deep])
    put_pair(0, act_part)


def pack(order, blocks, row_out, assign, tokens, pseudo, qe, qa, qg, ba, bg):
    half = len(order[0])
    width = tokens.shape[1] + pseudo.shape[1]
    cols = row_out // 2 * (ba.shape[1] + bg.shape[1])
    send = jax.ShapeDtypeStruct((2, CAP, width + 2 * cols), BF16)
    near = jax.ShapeDtypeStruct((2, CAP, width + cols), BF16)
    give = jax.ShapeDtypeStruct((half + 1, CAP, width + 2 * cols), BF16)
    operands = (assign, tokens, pseudo, qe, qa, qg, ba, bg)
    operands = tuple(pltpu.with_memory_space_constraint(x, pltpu.HBM) for x in operands)
    outs = pl.pallas_call(
        functools.partial(pack_kernel, order, blocks, row_out),
        out_shape=(send,) * half + (near,) * blocks + (give,),
        in_specs=[HBM] * len(operands),
        out_specs=(VMEM,) * (half + blocks + 1),
        scratch_shapes=[pltpu.VMEM(x.shape, x.dtype) for x in operands]
        + [pltpu.SemaphoreType.DMA((7 + CHUNKS,))],
        compiler_params=pltpu.CompilerParams(vmem_limit_bytes=32 * 1024 * 1024),
        name="select_rows_and_rotate_queries",
    )(*operands)
    return outs[:half], outs[half:-1], outs[-1]


def gather_kernel(*refs):
    *blocks, out_ref = refs
    width = out_ref.shape[1]
    out_ref[...] = jnp.concatenate([ref[c, :, :width] for ref in blocks for c in range(2)], axis=0)


def gather_rows(width, blocks):
    return pl.pallas_call(
        gather_kernel,
        out_shape=jax.ShapeDtypeStruct((2 * CAP * len(blocks), width), BF16),
        in_specs=[VMEM] * len(blocks),
        out_specs=VMEM,
        cost_estimate=pl.CostEstimate(flops=1000000000, bytes_accessed=8 * CAP * len(blocks) * width, transcendentals=0),
        name="gather_rows",
    )(*blocks)


def row_steps(rows):
    return [(i * 128, 64 if i < 2 else 128) for i in range(rows // 128)]


def factor_kernel(act_width, row_out, rounds, blocks, count_ref, *refs):
    here, there = refs[:rounds], refs[rounds : 2 * rounds]
    refs = refs[2 * rounds :]
    near, ready_ref = refs[:blocks], refs[blocks]
    refs = refs[1:]
    act_hbm, grad_hbm, rot_act_hbm, rot_grad_hbm = refs[blocks : blocks + 4]
    right_ref, act_ref, grad_ref, rot_act_ref, rot_grad_ref, sems = refs[blocks + 4 :]
    block, core = lax.axis_index("dp"), lax.axis_index("mp")
    act_block, act_half = act_ref.shape
    grad_block, grad_half = grad_ref.shape
    inverse = 1.0 / count_ref[0].astype(F32)
    contract = (((0,), (0,)), ((), ()))
    copies = []

    def send(src, dst):
        copy = pltpu.make_async_copy(src, dst, sems.at[len(copies)])
        copy.start()
        copies.append(copy)

    def columns(at, width):
        span = pl.ds(pl.multiple_of(at, 128), width)
        late = [ref[c, :, span] for ref in there for c in range(2)]
        return jnp.concatenate([ready_ref[:, span]] + late, axis=0)

    def tile(left, right):
        part = lax.dot_general(left, right, contract, preferred_element_type=F32)
        return (part * inverse).astype(BF16)

    right_ref[...] = columns(core * act_half, act_half)
    for first, step in row_steps(act_block):
        left = columns(block * act_block + first, 128)
        for at in range(0, 128, step):
            rows = pl.ds(first + at, step)
            act_ref[rows, :] = tile(left[:, at : at + step], right_ref[...])
            send(act_ref.at[rows], act_hbm.at[rows])

    grad_ref[...] = tile(
        columns(act_width + block * grad_block, grad_block),
        columns(act_width + core * grad_half, grad_half),
    )
    send(grad_ref, grad_hbm)

    act_cols = rot_act_ref.shape[1]
    cols = act_cols + rot_grad_ref.shape[1]
    base = act_width + 2 * grad_half
    for i in range(row_out // 2):
        total = jnp.zeros((2, cols), F32)
        at = base + i * 2 * cols
        for group, c in ((here, 0), (there, 1)):
            for ref in group:
                high = ref[c, :, at : at + cols].astype(F32)
                low = ref[c, :, at + cols : at + 2 * cols].astype(F32)
                total += high + low
        at = base + i * cols
        for ref in near:
            total += ref[0, :, at : at + cols].astype(F32) + ref[1, :, at : at + cols].astype(F32)
        rot_act_ref[2 * i : 2 * i + 2, :] = total[:, :act_cols].astype(BF16)
        rot_grad_ref[2 * i : 2 * i + 2, :] = total[:, act_cols:].astype(BF16)
    send(rot_act_ref, rot_act_hbm)
    send(rot_grad_ref, rot_grad_hbm)
    for copy in copies:
        copy.wait()


def factors(act_width, row_out, act_tile, grad_tile, act_cols, grad_cols, counts, here, there, near, ready):
    rounds, blocks = len(here), len(near)
    shapes = (act_tile, grad_tile, (row_out, act_cols), (row_out, grad_cols))
    return pl.pallas_call(
        functools.partial(factor_kernel, act_width, row_out, rounds, blocks),
        out_shape=tuple(jax.ShapeDtypeStruct(shape, BF16) for shape in shapes),
        in_specs=[SMEM] + [VMEM] * (2 * rounds + blocks + 1),
        out_specs=(HBM,) * 4,
        scratch_shapes=[pltpu.VMEM((2 * CAP * (2 * rounds + blocks), act_tile[1]), BF16)]
        + [pltpu.VMEM(shape, BF16) for shape in shapes]
        + [pltpu.SemaphoreType.DMA((act_tile[0] // 128 + 5,))],
        compiler_params=pltpu.CompilerParams(vmem_limit_bytes=40 * 1024 * 1024),
        name="factor_tiles",
    )(counts, *here, *there, *near, ready)


def local(
    tokens, pseudo, assign, counts, basis_act, basis_grad, queries_act, queries_grad, query_expert
):
    experts, blocks = lax.axis_size("expert"), lax.axis_size("dp")
    toks, d_model = tokens.shape
    slots, hidden = pseudo.shape[1], pseudo.shape[2]
    row_out = query_expert.shape[0] // (experts * blocks)
    order = partner_order(experts, blocks)
    half = len(order[0])
    sends, nears, give = pack(
        order,
        blocks,
        row_out,
        assign.T,
        tokens,
        pseudo.reshape(toks * slots, hidden),
        query_expert.T,
        queries_act,
        queries_grad,
        basis_act[0],
        basis_grad[0],
    )
    swap = [(0, 1), (1, 0)]
    got = lax.ppermute(give, "mp", swap)
    width = d_model + hidden
    nears = [near.at[1, :, :width].set(got[half, :, :width]) for near in nears]
    for dd in range(1, blocks):
        nears[dd] = lax.ppermute(nears[dd], "dp", [(d, d ^ dd) for d in range(blocks)])
    here = []
    for r in reversed(range(half)):
        pairs = [
            ((e * blocks + d) * 2 + m, ((e ^ order[m][r][0]) * blocks + (d ^ order[m][r][1])) * 2 + m)
            for e in range(experts)
            for d in range(blocks)
            for m in range(2)
        ]
        here.append(lax.ppermute(sends[r].at[1].set(got[r]), ("expert", "dp", "mp"), pairs))
    there = [lax.ppermute(rows, "mp", swap) for rows in here]
    act_cov, grad_cov, rot_act, rot_grad = factors(
        d_model,
        row_out,
        (d_model // blocks, d_model // 2),
        (hidden // blocks, hidden // 2),
        basis_act.shape[2],
        basis_grad.shape[2],
        counts,
        here,
        there,
        nears,
        gather_rows(width, here + nears),
    )
    return act_cov[None], grad_cov[None], rot_act, rot_grad


def solution(mesh):
    return jax.shard_map(
        local,
        mesh=mesh,
        in_specs=(
            P(("groups", "expert", "dp", "mp"), None),
            P(("groups", "expert", "dp", "mp"), None, None),
            P(("groups", "expert", "dp", "mp"), None),
            P(("groups", "expert")),
            P(("groups", "expert"), "dp", "mp"),
            P(("groups", "expert"), "dp", "mp"),
            P("groups", "dp"),
            P("groups", "dp"),
            P("groups", None),
        ),
        out_specs=(
            P(("groups", "expert"), "dp", "mp"),
            P(("groups", "expert"), "dp", "mp"),
            P(("groups", "expert", "dp"), "mp"),
            P(("groups", "expert", "dp"), "mp"),
        ),
        check_vma=False,
    )
```

```python
import functools

import jax
import jax.numpy as jnp
from jax import lax
from jax.experimental import pallas as pl
from jax.experimental.pallas import tpu as pltpu
from jax.sharding import PartitionSpec as P

CAP = 2
CHUNKS = 8
F32 = jnp.float32
BF16 = jnp.bfloat16
HBM = pl.BlockSpec(memory_space=pltpu.HBM)
VMEM = pl.BlockSpec(memory_space=pltpu.VMEM)
SMEM = pl.BlockSpec(memory_space=pltpu.SMEM)


def partner_order(experts, blocks):
    far = list(range(experts // 2, experts)) + list(range(experts // 2 - 1, 0, -1))
    return tuple([(de, dd) for de in far for dd in range(core, blocks, 2)] for core in range(2))


def dot(a, b):
    return jnp.dot(a, b, preferred_element_type=F32)


def by_row(table, rows, per):
    index = lax.broadcasted_iota(jnp.int32, (rows, 1), 0) // per
    value = jnp.zeros((rows, 1), jnp.int32)
    for i, entry in enumerate(table):
        if entry:
            value = jnp.where(index == i, entry, value)
    return value


def pack_kernel(order, blocks, row_out, *refs):
    assign_hbm, tokens_hbm, pseudo_hbm, qe_hbm, qa_hbm, qg_hbm, ba_hbm, bg_hbm = refs[:8]
    half = len(order[0])
    send_refs, near_refs, give_ref = refs[8 : 8 + half], refs[8 + half : 8 + half + blocks], refs[8 + half + blocks]
    assign_ref, tokens_ref, pseudo_ref, qe_ref, qa_ref, qg_ref, ba_ref, bg_ref, sems = refs[9 + half + blocks :]
    chunks = CHUNKS
    deep = ba_ref.shape[0] // chunks
    small = [
        pltpu.make_async_copy(src, dst, sems.at[i])
        for i, (src, dst) in enumerate(
            [
                (assign_hbm, assign_ref),
                (qe_hbm, qe_ref),
                (qa_hbm, qa_ref),
                (qg_hbm, qg_ref),
                (tokens_hbm, tokens_ref),
                (pseudo_hbm, pseudo_ref),
                (bg_hbm, bg_ref),
            ]
        )
    ]
    large = [
        pltpu.make_async_copy(
            ba_hbm.at[pl.ds(i * deep, deep)], ba_ref.at[pl.ds(i * deep, deep)], sems.at[len(small) + i]
        )
        for i in range(chunks)
    ]
    for copy in small + large:
        copy.start()
    expert, block, core = lax.axis_index("expert"), lax.axis_index("dp"), lax.axis_index("mp")
    rows = 2 * (2 * half + blocks)
    slots, toks = assign_ref.shape
    flat = slots * toks
    d_model, hidden = tokens_ref.shape[1], pseudo_ref.shape[1]
    same_expert = [(0, dd) for dd in range(blocks)]
    plan = [order[0] + order[1] + same_expert, order[1] + order[0] + same_expert]
    step_e = jnp.where(core == 0, by_row([p[0] for p in plan[0]], rows, 2), by_row([p[0] for p in plan[1]], rows, 2))
    step_d = jnp.where(core == 0, by_row([p[1] for p in plan[0]], rows, 2), by_row([p[1] for p in plan[1]], rows, 2))
    to_e, to_d = step_e ^ expert, step_d ^ block
    second = lax.broadcasted_iota(jnp.int32, (rows, 1), 0) % 2

    small[0].wait()
    spread = (
        lax.broadcasted_iota(jnp.int32, (toks, flat), 0)
        == lax.broadcasted_iota(jnp.int32, (toks, flat), 1) // slots
    ).astype(F32)
    ids = dot(assign_ref[...].astype(F32), spread)
    mine = (
        lax.broadcasted_iota(jnp.int32, (slots, flat), 0)
        == lax.broadcasted_iota(jnp.int32, (slots, flat), 1) % slots
    )
    ids = jnp.sum(jnp.where(mine, ids, 0.0), axis=0, keepdims=True).astype(jnp.int32)
    place = lax.broadcasted_iota(jnp.int32, (rows, flat), 1)
    hit = ids == to_e
    first = jnp.min(jnp.where(hit, place, flat), axis=1, keepdims=True)
    last = jnp.max(jnp.where(hit, place, -1), axis=1, keepdims=True)
    chosen = jnp.where(second == 0, first, jnp.where(last == first, -1, last))
    slot_pick = (place == chosen).astype(BF16)
    low = lax.broadcasted_iota(jnp.int32, (rows, toks), 1) * slots
    token_pick = ((chosen >= low) & (chosen < low + slots)).astype(BF16)

    def put(column, value):
        width = value.shape[1]
        for i in range(half):
            send_refs[i][0, :, column : column + width] = value[2 * i : 2 * i + 2]
            give_ref[i, :, column : column + width] = value[2 * (half + i) : 2 * (half + i) + 2]

    def put_rows(column, value):
        value = value.astype(BF16)
        put(column, value)
        width = value.shape[1]
        mine = value[4 * half : 4 * half + 2]
        give_ref[half, :, column : column + width] = mine
        for ref in near_refs:
            ref[0, :, column : column + width] = mine

    small[4].wait()
    put_rows(0, dot(token_pick, tokens_ref[...]))
    small[5].wait()
    put_rows(d_model, dot(slot_pick, pseudo_ref[...]))

    for i in (1, 2, 3):
        small[i].wait()
    queries = qa_ref.shape[0]
    base = d_model + hidden
    act_cols, grad_cols = ba_ref.shape[1], bg_ref.shape[1]
    asked = qe_ref[...] == expert
    query = lax.broadcasted_iota(jnp.int32, (rows, queries), 1)
    picks = []
    for i in range(row_out // 2):
        picks.append(
            ((query == (to_e * blocks + to_d) * row_out + 2 * i + second) & asked).astype(BF16)
        )
    pick = jnp.concatenate(picks, axis=0) if len(picks) > 1 else picks[0]
    my_act = dot(pick, qa_ref[...]).astype(BF16)
    my_grad = dot(pick, qg_ref[...]).astype(BF16)
    cols = act_cols + grad_cols

    def put_pair(column, value):
        high = value.astype(BF16)
        low = (value - high.astype(F32)).astype(BF16)
        width = value.shape[1]
        for i in range(row_out // 2):
            at = base + 2 * i * cols + column
            put(at, high[i * rows : (i + 1) * rows])
            put(at + cols, low[i * rows : (i + 1) * rows])
            at = base + i * cols + column
            for dd, ref in enumerate(near_refs):
                first = i * rows + 4 * half + 2 * dd
                ref[0, :, at : at + width] = high[first : first + 2]
                ref[1, :, at : at + width] = low[first : first + 2]

    small[6].wait()
    put_pair(act_cols, dot(my_grad, bg_ref[...]))
    act_part = jnp.zeros((my_act.shape[0], act_cols), F32)
    for c in range(chunks):
        large[c].wait()
        act_part += dot(my_act[:, c * deep : (c + 1) * deep], ba_ref[c * deep : (c + 1) * deep])
    put_pair(0, act_part)


def pack(order, blocks, row_out, assign, tokens, pseudo, qe, qa, qg, ba, bg):
    half = len(order[0])
    width = tokens.shape[1] + pseudo.shape[1]
    cols = row_out // 2 * (ba.shape[1] + bg.shape[1])
    send = jax.ShapeDtypeStruct((2, CAP, width + 2 * cols), BF16)
    near = jax.ShapeDtypeStruct((2, CAP, width + cols), BF16)
    give = jax.ShapeDtypeStruct((half + 1, CAP, width + 2 * cols), BF16)
    operands = (assign, tokens, pseudo, qe, qa, qg, ba, bg)
    operands = tuple(pltpu.with_memory_space_constraint(x, pltpu.HBM) for x in operands)
    outs = pl.pallas_call(
        functools.partial(pack_kernel, order, blocks, row_out),
        out_shape=(send,) * half + (near,) * blocks + (give,),
        in_specs=[HBM] * len(operands),
        out_specs=(VMEM,) * (half + blocks + 1),
        scratch_shapes=[pltpu.VMEM(x.shape, x.dtype) for x in operands]
        + [pltpu.SemaphoreType.DMA((7 + CHUNKS,))],
        compiler_params=pltpu.CompilerParams(vmem_limit_bytes=32 * 1024 * 1024),
        name="select_rows_and_rotate_queries",
    )(*operands)
    return outs[:half], outs[half:-1], outs[-1]


def gather_kernel(*refs):
    *blocks, out_ref = refs
    width = out_ref.shape[1]
    out_ref[...] = jnp.concatenate([ref[c, :, :width] for ref in blocks for c in range(2)], axis=0)


def gather_rows(width, blocks):
    return pl.pallas_call(
        gather_kernel,
        out_shape=jax.ShapeDtypeStruct((2 * CAP * len(blocks), width), BF16),
        in_specs=[VMEM] * len(blocks),
        out_specs=VMEM,
        compiler_params=pltpu.CompilerParams(vmem_limit_bytes=(2 << 20) + 16 * CAP * len(blocks) * width),
        cost_estimate=pl.CostEstimate(flops=1000000000, bytes_accessed=8 * CAP * len(blocks) * width, transcendentals=0),
        name="gather_rows",
    )(*blocks)


def row_steps(rows):
    return [(i * 128, 64 if i < 2 else 128) for i in range(rows // 128)]


def factor_kernel(act_width, row_out, rounds, blocks, count_ref, *refs):
    here, there = refs[:rounds], refs[rounds : 2 * rounds]
    refs = refs[2 * rounds :]
    near, ready_ref = refs[:blocks], refs[blocks]
    refs = refs[1:]
    act_hbm, grad_hbm, rot_act_hbm, rot_grad_hbm = refs[blocks : blocks + 4]
    right_ref, act_ref, grad_ref, rot_act_ref, rot_grad_ref, sems = refs[blocks + 4 :]
    block, core = lax.axis_index("dp"), lax.axis_index("mp")
    act_block, act_half = act_ref.shape
    grad_block, grad_half = grad_ref.shape
    inverse = 1.0 / count_ref[0].astype(F32)
    contract = (((0,), (0,)), ((), ()))
    copies = []

    def send(src, dst):
        copy = pltpu.make_async_copy(src, dst, sems.at[len(copies)])
        copy.start()
        copies.append(copy)

    def columns(at, width):
        span = pl.ds(pl.multiple_of(at, 128), width)
        late = [ref[c, :, span] for ref in there for c in range(2)]
        return jnp.concatenate([ready_ref[:, span]] + late, axis=0)

    def tile(left, right):
        part = lax.dot_general(left, right, contract, preferred_element_type=F32)
        return (part * inverse).astype(BF16)

    right_ref[...] = columns(core * act_half, act_half)
    for first, step in row_steps(act_block):
        left = columns(block * act_block + first, 128)
        for at in range(0, 128, step):
            rows = pl.ds(first + at, step)
            act_ref[rows, :] = tile(left[:, at : at + step], right_ref[...])
            send(act_ref.at[rows], act_hbm.at[rows])

    grad_ref[...] = tile(
        columns(act_width + block * grad_block, grad_block),
        columns(act_width + core * grad_half, grad_half),
    )
    send(grad_ref, grad_hbm)

    act_cols = rot_act_ref.shape[1]
    cols = act_cols + rot_grad_ref.shape[1]
    base = act_width + 2 * grad_half
    for i in range(row_out // 2):
        total = jnp.zeros((2, cols), F32)
        at = base + i * 2 * cols
        for group, c in ((here, 0), (there, 1)):
            for ref in group:
                high = ref[c, :, at : at + cols].astype(F32)
                low = ref[c, :, at + cols : at + 2 * cols].astype(F32)
                total += high + low
        at = base + i * cols
        for ref in near:
            total += ref[0, :, at : at + cols].astype(F32) + ref[1, :, at : at + cols].astype(F32)
        rot_act_ref[2 * i : 2 * i + 2, :] = total[:, :act_cols].astype(BF16)
        rot_grad_ref[2 * i : 2 * i + 2, :] = total[:, act_cols:].astype(BF16)
    send(rot_act_ref, rot_act_hbm)
    send(rot_grad_ref, rot_grad_hbm)
    for copy in copies:
        copy.wait()


def factors(act_width, row_out, act_tile, grad_tile, act_cols, grad_cols, counts, here, there, near, ready):
    rounds, blocks = len(here), len(near)
    shapes = (act_tile, grad_tile, (row_out, act_cols), (row_out, grad_cols))
    return pl.pallas_call(
        functools.partial(factor_kernel, act_width, row_out, rounds, blocks),
        out_shape=tuple(jax.ShapeDtypeStruct(shape, BF16) for shape in shapes),
        in_specs=[SMEM] + [VMEM] * (2 * rounds + blocks + 1),
        out_specs=(HBM,) * 4,
        scratch_shapes=[pltpu.VMEM((2 * CAP * (2 * rounds + blocks), act_tile[1]), BF16)]
        + [pltpu.VMEM(shape, BF16) for shape in shapes]
        + [pltpu.SemaphoreType.DMA((act_tile[0] // 128 + 5,))],
        compiler_params=pltpu.CompilerParams(vmem_limit_bytes=40 * 1024 * 1024),
        name="factor_tiles",
    )(counts, *here, *there, *near, ready)


def local(
    tokens, pseudo, assign, counts, basis_act, basis_grad, queries_act, queries_grad, query_expert
):
    experts, blocks = lax.axis_size("expert"), lax.axis_size("dp")
    toks, d_model = tokens.shape
    slots, hidden = pseudo.shape[1], pseudo.shape[2]
    row_out = query_expert.shape[0] // (experts * blocks)
    order = partner_order(experts, blocks)
    half = len(order[0])
    sends, nears, give = pack(
        order,
        blocks,
        row_out,
        assign.T,
        tokens,
        pseudo.reshape(toks * slots, hidden),
        query_expert.T,
        queries_act,
        queries_grad,
        basis_act[0],
        basis_grad[0],
    )
    swap = [(0, 1), (1, 0)]
    got = lax.ppermute(give, "mp", swap)
    width = d_model + hidden
    nears = [near.at[1, :, :width].set(got[half, :, :width]) for near in nears]
    for dd in range(1, blocks):
        nears[dd] = lax.ppermute(nears[dd], "dp", [(d, d ^ dd) for d in range(blocks)])
    here = []
    for r in reversed(range(half)):
        pairs = [
            ((e * blocks + d) * 2 + m, ((e ^ order[m][r][0]) * blocks + (d ^ order[m][r][1])) * 2 + m)
            for e in range(experts)
            for d in range(blocks)
            for m in range(2)
        ]
        here.append(lax.ppermute(sends[r].at[1].set(got[r]), ("expert", "dp", "mp"), pairs))
    there = [lax.ppermute(rows, "mp", swap) for rows in here]
    act_cov, grad_cov, rot_act, rot_grad = factors(
        d_model,
        row_out,
        (d_model // blocks, d_model // 2),
        (hidden // blocks, hidden // 2),
        basis_act.shape[2],
        basis_grad.shape[2],
        counts,
        here,
        there,
        nears,
        gather_rows(width, here + nears),
    )
    return act_cov[None], grad_cov[None], rot_act, rot_grad


def solution(mesh):
    return jax.shard_map(
        local,
        mesh=mesh,
        in_specs=(
            P(("groups", "expert", "dp", "mp"), None),
            P(("groups", "expert", "dp", "mp"), None, None),
            P(("groups", "expert", "dp", "mp"), None),
            P(("groups", "expert")),
            P(("groups", "expert"), "dp", "mp"),
            P(("groups", "expert"), "dp", "mp"),
            P("groups", "dp"),
            P("groups", "dp"),
            P("groups", None),
        ),
        out_specs=(
            P(("groups", "expert"), "dp", "mp"),
            P(("groups", "expert"), "dp", "mp"),
            P(("groups", "expert", "dp"), "mp"),
            P(("groups", "expert", "dp"), "mp"),
        ),
        check_vma=False,
    )
```

```python
import functools

import jax
import jax.numpy as jnp
from jax import lax
from jax.experimental import pallas as pl
from jax.experimental.pallas import tpu as pltpu
from jax.sharding import PartitionSpec as P

CAP = 2
CHUNKS = 8
F32 = jnp.float32
BF16 = jnp.bfloat16
HBM = pl.BlockSpec(memory_space=pltpu.HBM)
VMEM = pl.BlockSpec(memory_space=pltpu.VMEM)
SMEM = pl.BlockSpec(memory_space=pltpu.SMEM)


def partner_order(experts, blocks):
    far = list(range(experts // 2, experts)) + list(range(experts // 2 - 1, 0, -1))
    return tuple([(de, dd) for de in far for dd in range(core, blocks, 2)] for core in range(2))


def dot(a, b):
    return jnp.dot(a, b, preferred_element_type=F32)


def by_row(table, rows, per):
    index = lax.broadcasted_iota(jnp.int32, (rows, 1), 0) // per
    value = jnp.zeros((rows, 1), jnp.int32)
    for i, entry in enumerate(table):
        if entry:
            value = jnp.where(index == i, entry, value)
    return value


def pack_kernel(order, blocks, row_out, *refs):
    assign_hbm, tokens_hbm, pseudo_hbm, qe_hbm, qa_hbm, qg_hbm, ba_hbm, bg_hbm = refs[:8]
    half = len(order[0])
    send_refs, near_refs, give_ref = refs[8 : 8 + half], refs[8 + half : 8 + half + blocks], refs[8 + half + blocks]
    assign_ref, tokens_ref, pseudo_ref, qe_ref, qa_ref, qg_ref, ba_ref, bg_ref, sems = refs[9 + half + blocks :]
    chunks = CHUNKS
    deep = ba_ref.shape[0] // chunks
    small = [
        pltpu.make_async_copy(src, dst, sems.at[i])
        for i, (src, dst) in enumerate(
            [
                (assign_hbm, assign_ref),
                (qe_hbm, qe_ref),
                (qa_hbm, qa_ref),
                (qg_hbm, qg_ref),
                (tokens_hbm, tokens_ref),
                (pseudo_hbm, pseudo_ref),
                (bg_hbm, bg_ref),
            ]
        )
    ]
    large = [
        pltpu.make_async_copy(
            ba_hbm.at[pl.ds(i * deep, deep)], ba_ref.at[pl.ds(i * deep, deep)], sems.at[len(small) + i]
        )
        for i in range(chunks)
    ]
    for copy in small + large:
        copy.start()
    expert, block, core = lax.axis_index("expert"), lax.axis_index("dp"), lax.axis_index("mp")
    rows = 2 * (2 * half + blocks)
    slots, toks = assign_ref.shape
    flat = slots * toks
    d_model, hidden = tokens_ref.shape[1], pseudo_ref.shape[1]
    same_expert = [(0, dd) for dd in range(blocks)]
    plan = [order[0] + order[1] + same_expert, order[1] + order[0] + same_expert]
    step_e = jnp.where(core == 0, by_row([p[0] for p in plan[0]], rows, 2), by_row([p[0] for p in plan[1]], rows, 2))
    step_d = jnp.where(core == 0, by_row([p[1] for p in plan[0]], rows, 2), by_row([p[1] for p in plan[1]], rows, 2))
    to_e, to_d = step_e ^ expert, step_d ^ block
    second = lax.broadcasted_iota(jnp.int32, (rows, 1), 0) % 2

    small[0].wait()
    spread = (
        lax.broadcasted_iota(jnp.int32, (toks, flat), 0)
        == lax.broadcasted_iota(jnp.int32, (toks, flat), 1) // slots
    ).astype(F32)
    ids = dot(assign_ref[...].astype(F32), spread)
    mine = (
        lax.broadcasted_iota(jnp.int32, (slots, flat), 0)
        == lax.broadcasted_iota(jnp.int32, (slots, flat), 1) % slots
    )
    ids = jnp.sum(jnp.where(mine, ids, 0.0), axis=0, keepdims=True).astype(jnp.int32)
    place = lax.broadcasted_iota(jnp.int32, (rows, flat), 1)
    hit = ids == to_e
    first = jnp.min(jnp.where(hit, place, flat), axis=1, keepdims=True)
    last = jnp.max(jnp.where(hit, place, -1), axis=1, keepdims=True)
    chosen = jnp.where(second == 0, first, jnp.where(last == first, -1, last))
    slot_pick = (place == chosen).astype(BF16)
    low = lax.broadcasted_iota(jnp.int32, (rows, toks), 1) * slots
    token_pick = ((chosen >= low) & (chosen < low + slots)).astype(BF16)

    def put(column, value):
        width = value.shape[1]
        for i in range(half):
            send_refs[i][0, :, column : column + width] = value[2 * i : 2 * i + 2]
            give_ref[i, :, column : column + width] = value[2 * (half + i) : 2 * (half + i) + 2]

    def put_rows(column, value):
        value = value.astype(BF16)
        put(column, value)
        width = value.shape[1]
        mine = value[4 * half : 4 * half + 2]
        give_ref[half, :, column : column + width] = mine
        for ref in near_refs:
            ref[0, :, column : column + width] = mine

    small[4].wait()
    put_rows(0, dot(token_pick, tokens_ref[...]))
    small[5].wait()
    put_rows(d_model, dot(slot_pick, pseudo_ref[...]))

    for i in (1, 2, 3):
        small[i].wait()
    queries = qa_ref.shape[0]
    base = d_model + hidden
    act_cols, grad_cols = ba_ref.shape[1], bg_ref.shape[1]
    asked = qe_ref[...] == expert
    query = lax.broadcasted_iota(jnp.int32, (rows, queries), 1)
    picks = []
    for i in range(row_out // 2):
        picks.append(
            ((query == (to_e * blocks + to_d) * row_out + 2 * i + second) & asked).astype(BF16)
        )
    pick = jnp.concatenate(picks, axis=0) if len(picks) > 1 else picks[0]
    my_act = dot(pick, qa_ref[...]).astype(BF16)
    my_grad = dot(pick, qg_ref[...]).astype(BF16)
    cols = act_cols + grad_cols

    def put_pair(column, value):
        high = value.astype(BF16)
        low = (value - high.astype(F32)).astype(BF16)
        width = value.shape[1]
        for i in range(row_out // 2):
            at = base + 2 * i * cols + column
            put(at, high[i * rows : (i + 1) * rows])
            put(at + cols, low[i * rows : (i + 1) * rows])
            at = base + i * cols + column
            for dd, ref in enumerate(near_refs):
                first = i * rows + 4 * half + 2 * dd
                ref[0, :, at : at + width] = high[first : first + 2]
                ref[1, :, at : at + width] = low[first : first + 2]

    small[6].wait()
    put_pair(act_cols, dot(my_grad, bg_ref[...]))
    act_part = jnp.zeros((my_act.shape[0], act_cols), F32)
    for c in range(chunks):
        large[c].wait()
        act_part += dot(my_act[:, c * deep : (c + 1) * deep], ba_ref[c * deep : (c + 1) * deep])
    put_pair(0, act_part)


def pack(order, blocks, row_out, assign, tokens, pseudo, qe, qa, qg, ba, bg):
    half = len(order[0])
    width = tokens.shape[1] + pseudo.shape[1]
    cols = row_out // 2 * (ba.shape[1] + bg.shape[1])
    send = jax.ShapeDtypeStruct((2, CAP, width + 2 * cols), BF16)
    near = jax.ShapeDtypeStruct((2, CAP, width + cols), BF16)
    give = jax.ShapeDtypeStruct((half + 1, CAP, width + 2 * cols), BF16)
    operands = (assign, tokens, pseudo, qe, qa, qg, ba, bg)
    operands = tuple(pltpu.with_memory_space_constraint(x, pltpu.HBM) for x in operands)
    outs = pl.pallas_call(
        functools.partial(pack_kernel, order, blocks, row_out),
        out_shape=(send,) * half + (near,) * blocks + (give,),
        in_specs=[HBM] * len(operands),
        out_specs=(VMEM,) * (half + blocks + 1),
        scratch_shapes=[pltpu.VMEM(x.shape, x.dtype) for x in operands]
        + [pltpu.SemaphoreType.DMA((7 + CHUNKS,))],
        compiler_params=pltpu.CompilerParams(vmem_limit_bytes=32 * 1024 * 1024),
        name="select_rows_and_rotate_queries",
    )(*operands)
    return outs[:half], outs[half:-1], outs[-1]


def gather_kernel(*refs):
    *blocks, out_ref = refs
    width = out_ref.shape[1]
    out_ref[...] = jnp.concatenate([ref[c, :, :width] for ref in blocks for c in range(2)], axis=0)


def gather_rows(width, blocks):
    return pl.pallas_call(
        gather_kernel,
        out_shape=jax.ShapeDtypeStruct((2 * CAP * len(blocks), width), BF16),
        in_specs=[VMEM] * len(blocks),
        out_specs=VMEM,
        compiler_params=pltpu.CompilerParams(vmem_limit_bytes=(2 << 20) + 16 * CAP * len(blocks) * width),
        cost_estimate=pl.CostEstimate(flops=1000000000, bytes_accessed=8 * CAP * len(blocks) * width, transcendentals=0),
        name="gather_rows",
    )(*blocks)


def row_steps(rows):
    return [(i * 128, 64 if i < 2 else 128) for i in range(rows // 128)]


def factor_kernel(act_width, row_out, rounds, blocks, count_ref, *refs):
    here, there = refs[:rounds], refs[rounds : 2 * rounds]
    refs = refs[2 * rounds :]
    near, ready_ref = refs[:blocks], refs[blocks]
    refs = refs[1:]
    act_hbm, grad_hbm, rot_act_hbm, rot_grad_hbm = refs[blocks : blocks + 4]
    right_ref, act_ref, grad_ref, rot_act_ref, rot_grad_ref, sems = refs[blocks + 4 :]
    block, core = lax.axis_index("dp"), lax.axis_index("mp")
    act_block, act_half = act_ref.shape
    grad_block, grad_half = grad_ref.shape
    inverse = 1.0 / count_ref[0].astype(F32)
    contract = (((0,), (0,)), ((), ()))
    copies = []

    def send(src, dst):
        copy = pltpu.make_async_copy(src, dst, sems.at[len(copies)])
        copy.start()
        copies.append(copy)

    def columns(at, width):
        extra = 64 if width % 128 else 0
        start = at - at % 128 if extra else at
        span = pl.ds(pl.multiple_of(start, 128), width + extra)
        late = [ref[c, :, span] for ref in there for c in range(2)]
        rows = jnp.concatenate([ready_ref[:, span]] + late, axis=0)
        if extra:
            rows = jnp.where(at % 128 == 0, rows[:, :width], rows[:, extra:])
        return rows

    def tile(left, right):
        part = lax.dot_general(left, right, contract, preferred_element_type=F32)
        return (part * inverse).astype(BF16)

    right_ref[...] = columns(core * act_half, act_half)
    for first, step in row_steps(act_block):
        left = columns(block * act_block + first, 128)
        for at in range(0, 128, step):
            rows = pl.ds(first + at, step)
            act_ref[rows, :] = tile(left[:, at : at + step], right_ref[...])
            send(act_ref.at[rows], act_hbm.at[rows])

    grad_ref[...] = tile(
        columns(act_width + block * grad_block, grad_block),
        columns(act_width + core * grad_half, grad_half),
    )
    send(grad_ref, grad_hbm)

    act_cols = rot_act_ref.shape[1]
    cols = act_cols + rot_grad_ref.shape[1]
    base = act_width + 2 * grad_half
    for i in range(row_out // 2):
        total = jnp.zeros((2, cols), F32)
        at = base + i * 2 * cols
        for group, c in ((here, 0), (there, 1)):
            for ref in group:
                high = ref[c, :, at : at + cols].astype(F32)
                low = ref[c, :, at + cols : at + 2 * cols].astype(F32)
                total += high + low
        at = base + i * cols
        for ref in near:
            total += ref[0, :, at : at + cols].astype(F32) + ref[1, :, at : at + cols].astype(F32)
        rot_act_ref[2 * i : 2 * i + 2, :] = total[:, :act_cols].astype(BF16)
        rot_grad_ref[2 * i : 2 * i + 2, :] = total[:, act_cols:].astype(BF16)
    send(rot_act_ref, rot_act_hbm)
    send(rot_grad_ref, rot_grad_hbm)
    for copy in copies:
        copy.wait()


def factors(act_width, row_out, act_tile, grad_tile, act_cols, grad_cols, counts, here, there, near, ready):
    rounds, blocks = len(here), len(near)
    shapes = (act_tile, grad_tile, (row_out, act_cols), (row_out, grad_cols))
    return pl.pallas_call(
        functools.partial(factor_kernel, act_width, row_out, rounds, blocks),
        out_shape=tuple(jax.ShapeDtypeStruct(shape, BF16) for shape in shapes),
        in_specs=[SMEM] + [VMEM] * (2 * rounds + blocks + 1),
        out_specs=(HBM,) * 4,
        scratch_shapes=[pltpu.VMEM((2 * CAP * (2 * rounds + blocks), act_tile[1]), BF16)]
        + [pltpu.VMEM(shape, BF16) for shape in shapes]
        + [pltpu.SemaphoreType.DMA((act_tile[0] // 128 + 5,))],
        compiler_params=pltpu.CompilerParams(vmem_limit_bytes=40 * 1024 * 1024),
        name="factor_tiles",
    )(counts, *here, *there, *near, ready)


def local(
    tokens, pseudo, assign, counts, basis_act, basis_grad, queries_act, queries_grad, query_expert
):
    experts, blocks = lax.axis_size("expert"), lax.axis_size("dp")
    toks, d_model = tokens.shape
    slots, hidden = pseudo.shape[1], pseudo.shape[2]
    row_out = query_expert.shape[0] // (experts * blocks)
    order = partner_order(experts, blocks)
    half = len(order[0])
    sends, nears, give = pack(
        order,
        blocks,
        row_out,
        assign.T,
        tokens,
        pseudo.reshape(toks * slots, hidden),
        query_expert.T,
        queries_act,
        queries_grad,
        basis_act[0],
        basis_grad[0],
    )
    swap = [(0, 1), (1, 0)]
    got = lax.ppermute(give, "mp", swap)
    width = d_model + hidden
    nears = [near.at[1, :, :width].set(got[half, :, :width]) for near in nears]
    for dd in range(1, blocks):
        nears[dd] = lax.ppermute(nears[dd], "dp", [(d, d ^ dd) for d in range(blocks)])
    here = []
    for r in reversed(range(half)):
        pairs = [
            ((e * blocks + d) * 2 + m, ((e ^ order[m][r][0]) * blocks + (d ^ order[m][r][1])) * 2 + m)
            for e in range(experts)
            for d in range(blocks)
            for m in range(2)
        ]
        here.append(lax.ppermute(sends[r].at[1].set(got[r]), ("expert", "dp", "mp"), pairs))
    there = [lax.ppermute(rows, "mp", swap) for rows in here]
    act_cov, grad_cov, rot_act, rot_grad = factors(
        d_model,
        row_out,
        (d_model // blocks, d_model // 2),
        (hidden // blocks, hidden // 2),
        basis_act.shape[2],
        basis_grad.shape[2],
        counts,
        here,
        there,
        nears,
        gather_rows(width, here + nears),
    )
    return act_cov[None], grad_cov[None], rot_act, rot_grad


def solution(mesh):
    return jax.shard_map(
        local,
        mesh=mesh,
        in_specs=(
            P(("groups", "expert", "dp", "mp"), None),
            P(("groups", "expert", "dp", "mp"), None, None),
            P(("groups", "expert", "dp", "mp"), None),
            P(("groups", "expert")),
            P(("groups", "expert"), "dp", "mp"),
            P(("groups", "expert"), "dp", "mp"),
            P("groups", "dp"),
            P("groups", "dp"),
            P("groups", None),
        ),
        out_specs=(
            P(("groups", "expert"), "dp", "mp"),
            P(("groups", "expert"), "dp", "mp"),
            P(("groups", "expert", "dp"), "mp"),
            P(("groups", "expert", "dp"), "mp"),
        ),
        check_vma=False,
    )
```

```python
import functools

import jax
import jax.numpy as jnp
from jax import lax
from jax.experimental import pallas as pl
from jax.experimental.pallas import tpu as pltpu
from jax.sharding import PartitionSpec as P

CAP = 2
CHUNKS = (3, 3, 3, 3, 2, 1, 1)
F32 = jnp.float32
BF16 = jnp.bfloat16
HBM = pl.BlockSpec(memory_space=pltpu.HBM)
VMEM = pl.BlockSpec(memory_space=pltpu.VMEM)
SMEM = pl.BlockSpec(memory_space=pltpu.SMEM)


def partner_order(experts, blocks):
    far = list(range(experts // 2, experts)) + list(range(experts // 2 - 1, 0, -1))
    return tuple([(de, dd) for de in far for dd in range(core, blocks, 2)] for core in range(2))


def dot(a, b):
    return jnp.dot(a, b, preferred_element_type=F32)


def by_row(table, rows, per):
    index = lax.broadcasted_iota(jnp.int32, (rows, 1), 0) // per
    value = jnp.zeros((rows, 1), jnp.int32)
    for i, entry in enumerate(table):
        if entry:
            value = jnp.where(index == i, entry, value)
    return value


def pack_kernel(order, blocks, row_out, *refs):
    assign_hbm, tokens_hbm, pseudo_hbm, qe_hbm, qa_hbm, qg_hbm, ba_hbm, bg_hbm = refs[:8]
    half = len(order[0])
    send_refs, near_refs, give_ref = refs[8 : 8 + half], refs[8 + half : 8 + half + blocks], refs[8 + half + blocks]
    assign_ref, tokens_ref, pseudo_ref, qe_ref, qa_ref, qg_ref, ba_ref, bg_ref, sems = refs[9 + half + blocks :]
    deep = ba_ref.shape[0] // sum(CHUNKS)
    spans = [(sum(CHUNKS[:i]) * deep, part * deep) for i, part in enumerate(CHUNKS)]
    small = [
        pltpu.make_async_copy(src, dst, sems.at[i])
        for i, (src, dst) in enumerate(
            [
                (assign_hbm, assign_ref),
                (qe_hbm, qe_ref),
                (qa_hbm, qa_ref),
                (qg_hbm, qg_ref),
                (tokens_hbm, tokens_ref),
                (pseudo_hbm, pseudo_ref),
                (bg_hbm, bg_ref),
            ]
        )
    ]
    large = [
        pltpu.make_async_copy(
            ba_hbm.at[pl.ds(at, size)], ba_ref.at[pl.ds(at, size)], sems.at[len(small) + i]
        )
        for i, (at, size) in enumerate(spans)
    ]
    for copy in small + large:
        copy.start()
    expert, block, core = lax.axis_index("expert"), lax.axis_index("dp"), lax.axis_index("mp")
    rows = 2 * (2 * half + blocks)
    slots, toks = assign_ref.shape
    flat = slots * toks
    d_model, hidden = tokens_ref.shape[1], pseudo_ref.shape[1]
    same_expert = [(0, dd) for dd in range(blocks)]
    plan = [order[0] + order[1] + same_expert, order[1] + order[0] + same_expert]
    step_e = jnp.where(core == 0, by_row([p[0] for p in plan[0]], rows, 2), by_row([p[0] for p in plan[1]], rows, 2))
    step_d = jnp.where(core == 0, by_row([p[1] for p in plan[0]], rows, 2), by_row([p[1] for p in plan[1]], rows, 2))
    to_e, to_d = step_e ^ expert, step_d ^ block
    second = lax.broadcasted_iota(jnp.int32, (rows, 1), 0) % 2

    small[0].wait()
    spread = (
        lax.broadcasted_iota(jnp.int32, (toks, flat), 0)
        == lax.broadcasted_iota(jnp.int32, (toks, flat), 1) // slots
    ).astype(F32)
    ids = dot(assign_ref[...].astype(F32), spread)
    mine = (
        lax.broadcasted_iota(jnp.int32, (slots, flat), 0)
        == lax.broadcasted_iota(jnp.int32, (slots, flat), 1) % slots
    )
    ids = jnp.sum(jnp.where(mine, ids, 0.0), axis=0, keepdims=True).astype(jnp.int32)
    place = lax.broadcasted_iota(jnp.int32, (rows, flat), 1)
    hit = ids == to_e
    first = jnp.min(jnp.where(hit, place, flat), axis=1, keepdims=True)
    last = jnp.max(jnp.where(hit, place, -1), axis=1, keepdims=True)
    chosen = jnp.where(second == 0, first, jnp.where(last == first, -1, last))
    slot_pick = (place == chosen).astype(BF16)
    low = lax.broadcasted_iota(jnp.int32, (rows, toks), 1) * slots
    token_pick = ((chosen >= low) & (chosen < low + slots)).astype(BF16)

    def put(column, value):
        width = value.shape[1]
        for i in range(half):
            send_refs[i][0, :, column : column + width] = value[2 * i : 2 * i + 2]
            give_ref[i, :, column : column + width] = value[2 * (half + i) : 2 * (half + i) + 2]

    def put_rows(column, value):
        value = value.astype(BF16)
        put(column, value)
        width = value.shape[1]
        mine = value[4 * half : 4 * half + 2]
        give_ref[half, :, column : column + width] = mine
        for ref in near_refs:
            ref[0, :, column : column + width] = mine

    small[4].wait()
    put_rows(0, dot(token_pick, tokens_ref[...]))
    small[5].wait()
    put_rows(d_model, dot(slot_pick, pseudo_ref[...]))

    for i in (1, 2, 3):
        small[i].wait()
    queries = qa_ref.shape[0]
    base = d_model + hidden
    act_cols, grad_cols = ba_ref.shape[1], bg_ref.shape[1]
    asked = qe_ref[...] == expert
    query = lax.broadcasted_iota(jnp.int32, (rows, queries), 1)
    picks = []
    for i in range(row_out // 2):
        picks.append(
            ((query == (to_e * blocks + to_d) * row_out + 2 * i + second) & asked).astype(BF16)
        )
    pick = jnp.concatenate(picks, axis=0) if len(picks) > 1 else picks[0]
    my_act = dot(pick, qa_ref[...]).astype(BF16)
    my_grad = dot(pick, qg_ref[...]).astype(BF16)
    cols = act_cols + grad_cols

    def put_pair(column, value):
        high = value.astype(BF16)
        low = (value - high.astype(F32)).astype(BF16)
        width = value.shape[1]
        for i in range(row_out // 2):
            at = base + 2 * i * cols + column
            put(at, high[i * rows : (i + 1) * rows])
            put(at + cols, low[i * rows : (i + 1) * rows])
            at = base + i * cols + column
            for dd, ref in enumerate(near_refs):
                first = i * rows + 4 * half + 2 * dd
                ref[0, :, at : at + width] = high[first : first + 2]
                ref[1, :, at : at + width] = low[first : first + 2]

    small[6].wait()
    put_pair(act_cols, dot(my_grad, bg_ref[...]))
    act_part = jnp.zeros((my_act.shape[0], act_cols), F32)
    for copy, (at, size) in zip(large, spans):
        copy.wait()
        act_part += dot(my_act[:, at : at + size], ba_ref[at : at + size])
    put_pair(0, act_part)


def pack(order, blocks, row_out, assign, tokens, pseudo, qe, qa, qg, ba, bg):
    half = len(order[0])
    width = tokens.shape[1] + pseudo.shape[1]
    cols = row_out // 2 * (ba.shape[1] + bg.shape[1])
    send = jax.ShapeDtypeStruct((2, CAP, width + 2 * cols), BF16)
    near = jax.ShapeDtypeStruct((2, CAP, width + cols), BF16)
    give = jax.ShapeDtypeStruct((half + 1, CAP, width + 2 * cols), BF16)
    operands = (assign, tokens, pseudo, qe, qa, qg, ba, bg)
    operands = tuple(pltpu.with_memory_space_constraint(x, pltpu.HBM) for x in operands)
    outs = pl.pallas_call(
        functools.partial(pack_kernel, order, blocks, row_out),
        out_shape=(send,) * half + (near,) * blocks + (give,),
        in_specs=[HBM] * len(operands),
        out_specs=(VMEM,) * (half + blocks + 1),
        scratch_shapes=[pltpu.VMEM(x.shape, x.dtype) for x in operands]
        + [pltpu.SemaphoreType.DMA((7 + len(CHUNKS),))],
        compiler_params=pltpu.CompilerParams(vmem_limit_bytes=32 * 1024 * 1024),
        name="select_rows_and_rotate_queries",
    )(*operands)
    return outs[:half], outs[half:-1], outs[-1]


def gather_kernel(*refs):
    *blocks, out_ref = refs
    width = out_ref.shape[1]
    out_ref[...] = jnp.concatenate([ref[c, :, :width] for ref in blocks for c in range(2)], axis=0)


def gather_rows(width, blocks):
    return pl.pallas_call(
        gather_kernel,
        out_shape=jax.ShapeDtypeStruct((2 * CAP * len(blocks), width), BF16),
        in_specs=[VMEM] * len(blocks),
        out_specs=VMEM,
        compiler_params=pltpu.CompilerParams(vmem_limit_bytes=(2 << 20) + 16 * CAP * len(blocks) * width),
        cost_estimate=pl.CostEstimate(flops=1000000000, bytes_accessed=8 * CAP * len(blocks) * width, transcendentals=0),
        name="gather_rows",
    )(*blocks)


def row_steps(rows):
    return [(i * 128, 64 if i < 2 else 128) for i in range(rows // 128)]


def factor_kernel(act_width, row_out, rounds, blocks, count_ref, *refs):
    here, there = refs[:rounds], refs[rounds : 2 * rounds]
    refs = refs[2 * rounds :]
    near, ready_ref = refs[:blocks], refs[blocks]
    refs = refs[1:]
    act_hbm, grad_hbm, rot_act_hbm, rot_grad_hbm = refs[blocks : blocks + 4]
    right_ref, act_ref, grad_ref, rot_act_ref, rot_grad_ref, sems = refs[blocks + 4 :]
    block, core = lax.axis_index("dp"), lax.axis_index("mp")
    act_block, act_half = act_ref.shape
    grad_block, grad_half = grad_ref.shape
    inverse = 1.0 / count_ref[0].astype(F32)
    contract = (((0,), (0,)), ((), ()))
    copies = []

    def send(src, dst):
        copy = pltpu.make_async_copy(src, dst, sems.at[len(copies)])
        copy.start()
        copies.append(copy)

    def columns(at, width):
        extra = 64 if width % 128 else 0
        start = at - at % 128 if extra else at
        span = pl.ds(pl.multiple_of(start, 128), width + extra)
        late = [ref[c, :, span] for ref in there for c in range(2)]
        rows = jnp.concatenate([ready_ref[:, span]] + late, axis=0)
        if extra:
            rows = jnp.where(at % 128 == 0, rows[:, :width], rows[:, extra:])
        return rows

    def tile(left, right):
        part = lax.dot_general(left, right, contract, preferred_element_type=F32)
        return (part * inverse).astype(BF16)

    right_ref[...] = columns(core * act_half, act_half)
    for first, step in row_steps(act_block):
        left = columns(block * act_block + first, 128)
        for at in range(0, 128, step):
            rows = pl.ds(first + at, step)
            act_ref[rows, :] = tile(left[:, at : at + step], right_ref[...])
            send(act_ref.at[rows], act_hbm.at[rows])

    grad_ref[...] = tile(
        columns(act_width + block * grad_block, grad_block),
        columns(act_width + core * grad_half, grad_half),
    )
    send(grad_ref, grad_hbm)

    act_cols = rot_act_ref.shape[1]
    cols = act_cols + rot_grad_ref.shape[1]
    base = act_width + 2 * grad_half
    for i in range(row_out // 2):
        total = jnp.zeros((2, cols), F32)
        at = base + i * 2 * cols
        for group, c in ((here, 0), (there, 1)):
            for ref in group:
                high = ref[c, :, at : at + cols].astype(F32)
                low = ref[c, :, at + cols : at + 2 * cols].astype(F32)
                total += high + low
        at = base + i * cols
        for ref in near:
            total += ref[0, :, at : at + cols].astype(F32) + ref[1, :, at : at + cols].astype(F32)
        rot_act_ref[2 * i : 2 * i + 2, :] = total[:, :act_cols].astype(BF16)
        rot_grad_ref[2 * i : 2 * i + 2, :] = total[:, act_cols:].astype(BF16)
    send(rot_act_ref, rot_act_hbm)
    send(rot_grad_ref, rot_grad_hbm)
    for copy in copies:
        copy.wait()


def factors(act_width, row_out, act_tile, grad_tile, act_cols, grad_cols, counts, here, there, near, ready):
    rounds, blocks = len(here), len(near)
    shapes = (act_tile, grad_tile, (row_out, act_cols), (row_out, grad_cols))
    return pl.pallas_call(
        functools.partial(factor_kernel, act_width, row_out, rounds, blocks),
        out_shape=tuple(jax.ShapeDtypeStruct(shape, BF16) for shape in shapes),
        in_specs=[SMEM] + [VMEM] * (2 * rounds + blocks + 1),
        out_specs=(HBM,) * 4,
        scratch_shapes=[pltpu.VMEM((2 * CAP * (2 * rounds + blocks), act_tile[1]), BF16)]
        + [pltpu.VMEM(shape, BF16) for shape in shapes]
        + [pltpu.SemaphoreType.DMA((act_tile[0] // 128 + 5,))],
        compiler_params=pltpu.CompilerParams(vmem_limit_bytes=40 * 1024 * 1024),
        name="factor_tiles",
    )(counts, *here, *there, *near, ready)


def local(
    tokens, pseudo, assign, counts, basis_act, basis_grad, queries_act, queries_grad, query_expert
):
    experts, blocks = lax.axis_size("expert"), lax.axis_size("dp")
    toks, d_model = tokens.shape
    slots, hidden = pseudo.shape[1], pseudo.shape[2]
    row_out = query_expert.shape[0] // (experts * blocks)
    order = partner_order(experts, blocks)
    half = len(order[0])
    sends, nears, give = pack(
        order,
        blocks,
        row_out,
        assign.T,
        tokens,
        pseudo.reshape(toks * slots, hidden),
        query_expert.T,
        queries_act,
        queries_grad,
        basis_act[0],
        basis_grad[0],
    )
    swap = [(0, 1), (1, 0)]
    got = lax.ppermute(give, "mp", swap)
    width = d_model + hidden
    nears = [near.at[1, :, :width].set(got[half, :, :width]) for near in nears]
    for dd in range(1, blocks):
        nears[dd] = lax.ppermute(nears[dd], "dp", [(d, d ^ dd) for d in range(blocks)])
    here = []
    for r in reversed(range(half)):
        pairs = [
            ((e * blocks + d) * 2 + m, ((e ^ order[m][r][0]) * blocks + (d ^ order[m][r][1])) * 2 + m)
            for e in range(experts)
            for d in range(blocks)
            for m in range(2)
        ]
        here.append(lax.ppermute(sends[r].at[1].set(got[r]), ("expert", "dp", "mp"), pairs))
    there = [lax.ppermute(rows, "mp", swap) for rows in here]
    act_cov, grad_cov, rot_act, rot_grad = factors(
        d_model,
        row_out,
        (d_model // blocks, d_model // 2),
        (hidden // blocks, hidden // 2),
        basis_act.shape[2],
        basis_grad.shape[2],
        counts,
        here,
        there,
        nears,
        gather_rows(width, here + nears),
    )
    return act_cov[None], grad_cov[None], rot_act, rot_grad


def solution(mesh):
    return jax.shard_map(
        local,
        mesh=mesh,
        in_specs=(
            P(("groups", "expert", "dp", "mp"), None),
            P(("groups", "expert", "dp", "mp"), None, None),
            P(("groups", "expert", "dp", "mp"), None),
            P(("groups", "expert")),
            P(("groups", "expert"), "dp", "mp"),
            P(("groups", "expert"), "dp", "mp"),
            P("groups", "dp"),
            P("groups", "dp"),
            P("groups", None),
        ),
        out_specs=(
            P(("groups", "expert"), "dp", "mp"),
            P(("groups", "expert"), "dp", "mp"),
            P(("groups", "expert", "dp"), "mp"),
            P(("groups", "expert", "dp"), "mp"),
        ),
        check_vma=False,
    )
```

```python
import functools

import jax
import jax.numpy as jnp
from jax import lax
from jax.experimental import pallas as pl
from jax.experimental.pallas import tpu as pltpu
from jax.sharding import PartitionSpec as P

CAP = 2
CHUNKS = (3, 3, 3, 3, 2, 1, 1)
F32 = jnp.float32
BF16 = jnp.bfloat16
HBM = pl.BlockSpec(memory_space=pltpu.HBM)
VMEM = pl.BlockSpec(memory_space=pltpu.VMEM)
SMEM = pl.BlockSpec(memory_space=pltpu.SMEM)


def partner_order(experts, blocks):
    far = list(range(experts // 2, experts)) + list(range(experts // 2 - 1, 0, -1))
    return tuple([(de, dd) for de in far for dd in range(core, blocks, 2)] for core in range(2))


def dot(a, b):
    return jnp.dot(a, b, preferred_element_type=F32)


def by_row(table, rows, per):
    index = lax.broadcasted_iota(jnp.int32, (rows, 1), 0) // per
    value = jnp.zeros((rows, 1), jnp.int32)
    for i, entry in enumerate(table):
        if entry:
            value = jnp.where(index == i, entry, value)
    return value


def pack_kernel(order, blocks, row_out, *refs):
    assign_hbm, tokens_hbm, pseudo_hbm, qe_hbm, qa_hbm, qg_hbm, ba_hbm, bg_hbm = refs[:8]
    half = len(order[0])
    send_refs, near_refs, give_ref = refs[8 : 8 + half], refs[8 + half : 8 + half + blocks], refs[8 + half + blocks]
    assign_ref, tokens_ref, pseudo_ref, qe_ref, qa_ref, qg_ref, ba_ref, bg_ref, sems = refs[9 + half + blocks :]
    deep = ba_ref.shape[0] // sum(CHUNKS)
    spans = [(sum(CHUNKS[:i]) * deep, part * deep) for i, part in enumerate(CHUNKS)]
    small = [
        pltpu.make_async_copy(src, dst, sems.at[i])
        for i, (src, dst) in enumerate(
            [
                (assign_hbm, assign_ref),
                (qe_hbm, qe_ref),
                (qa_hbm, qa_ref),
                (qg_hbm, qg_ref),
                (tokens_hbm, tokens_ref),
                (pseudo_hbm, pseudo_ref),
                (bg_hbm, bg_ref),
            ]
        )
    ]
    large = [
        pltpu.make_async_copy(
            ba_hbm.at[pl.ds(at, size)], ba_ref.at[pl.ds(at, size)], sems.at[len(small) + i]
        )
        for i, (at, size) in enumerate(spans)
    ]
    for copy in small + large:
        copy.start()
    expert, block, core = lax.axis_index("expert"), lax.axis_index("dp"), lax.axis_index("mp")
    rows = 2 * (2 * half + blocks)
    slots, toks = assign_ref.shape
    flat = slots * toks
    d_model, hidden = tokens_ref.shape[1], pseudo_ref.shape[1]
    same_expert = [(0, dd) for dd in range(blocks)]
    plan = [order[0] + order[1] + same_expert, order[1] + order[0] + same_expert]
    step_e = jnp.where(core == 0, by_row([p[0] for p in plan[0]], rows, 2), by_row([p[0] for p in plan[1]], rows, 2))
    step_d = jnp.where(core == 0, by_row([p[1] for p in plan[0]], rows, 2), by_row([p[1] for p in plan[1]], rows, 2))
    to_e, to_d = step_e ^ expert, step_d ^ block
    second = lax.broadcasted_iota(jnp.int32, (rows, 1), 0) % 2

    small[0].wait()
    spread = (
        lax.broadcasted_iota(jnp.int32, (toks, flat), 0)
        == lax.broadcasted_iota(jnp.int32, (toks, flat), 1) // slots
    ).astype(F32)
    ids = dot(assign_ref[...].astype(F32), spread)
    mine = (
        lax.broadcasted_iota(jnp.int32, (slots, flat), 0)
        == lax.broadcasted_iota(jnp.int32, (slots, flat), 1) % slots
    )
    ids = jnp.sum(jnp.where(mine, ids, 0.0), axis=0, keepdims=True).astype(jnp.int32)
    place = lax.broadcasted_iota(jnp.int32, (rows, flat), 1)
    hit = ids == to_e
    first = jnp.min(jnp.where(hit, place, flat), axis=1, keepdims=True)
    last = jnp.max(jnp.where(hit, place, -1), axis=1, keepdims=True)
    chosen = jnp.where(second == 0, first, jnp.where(last == first, -1, last))
    slot_pick = (place == chosen).astype(BF16)
    low = lax.broadcasted_iota(jnp.int32, (rows, toks), 1) * slots
    token_pick = ((chosen >= low) & (chosen < low + slots)).astype(BF16)

    def put(column, value):
        width = value.shape[1]
        for i in range(half):
            send_refs[i][0, :, column : column + width] = value[2 * i : 2 * i + 2]
            give_ref[i, :, column : column + width] = value[2 * (half + i) : 2 * (half + i) + 2]

    def put_rows(column, value):
        value = value.astype(BF16)
        put(column, value)
        width = value.shape[1]
        mine = value[4 * half : 4 * half + 2]
        give_ref[half, :, column : column + width] = mine
        for ref in near_refs:
            ref[0, :, column : column + width] = mine

    small[4].wait()
    put_rows(0, dot(token_pick, tokens_ref[...]))
    small[5].wait()
    put_rows(d_model, dot(slot_pick, pseudo_ref[...]))

    for i in (1, 2, 3):
        small[i].wait()
    queries = qa_ref.shape[0]
    base = d_model + hidden
    act_cols, grad_cols = ba_ref.shape[1], bg_ref.shape[1]
    asked = qe_ref[...] == expert
    query = lax.broadcasted_iota(jnp.int32, (rows, queries), 1)
    picks = []
    for i in range(row_out // 2):
        picks.append(
            ((query == (to_e * blocks + to_d) * row_out + 2 * i + second) & asked).astype(BF16)
        )
    pick = jnp.concatenate(picks, axis=0) if len(picks) > 1 else picks[0]
    my_act = dot(pick, qa_ref[...]).astype(BF16)
    my_grad = dot(pick, qg_ref[...]).astype(BF16)
    cols = act_cols + grad_cols

    def put_pair(column, value):
        high = value.astype(BF16)
        low = (value - high.astype(F32)).astype(BF16)
        width = value.shape[1]
        for i in range(row_out // 2):
            at = base + 2 * i * cols + column
            put(at, high[i * rows : (i + 1) * rows])
            put(at + cols, low[i * rows : (i + 1) * rows])
            at = base + i * cols + column
            for dd, ref in enumerate(near_refs):
                first = i * rows + 4 * half + 2 * dd
                ref[0, :, at : at + width] = high[first : first + 2]
                ref[1, :, at : at + width] = low[first : first + 2]

    small[6].wait()
    put_pair(act_cols, dot(my_grad, bg_ref[...]))
    act_part = jnp.zeros((my_act.shape[0], act_cols), F32)
    for copy, (at, size) in zip(large, spans):
        copy.wait()
        act_part += dot(my_act[:, at : at + size], ba_ref[at : at + size])
    put_pair(0, act_part)


def pack(order, blocks, row_out, assign, tokens, pseudo, qe, qa, qg, ba, bg):
    half = len(order[0])
    width = tokens.shape[1] + pseudo.shape[1]
    cols = row_out // 2 * (ba.shape[1] + bg.shape[1])
    send = jax.ShapeDtypeStruct((2, CAP, width + 2 * cols), BF16)
    near = jax.ShapeDtypeStruct((2, CAP, width + cols), BF16)
    give = jax.ShapeDtypeStruct((half + 1, CAP, width + 2 * cols), BF16)
    operands = (assign, tokens, pseudo, qe, qa, qg, ba, bg)
    operands = tuple(pltpu.with_memory_space_constraint(x, pltpu.HBM) for x in operands)
    outs = pl.pallas_call(
        functools.partial(pack_kernel, order, blocks, row_out),
        out_shape=(send,) * half + (near,) * blocks + (give,),
        in_specs=[HBM] * len(operands),
        out_specs=(VMEM,) * (half + blocks + 1),
        scratch_shapes=[pltpu.VMEM(x.shape, x.dtype) for x in operands]
        + [pltpu.SemaphoreType.DMA((7 + len(CHUNKS),))],
        compiler_params=pltpu.CompilerParams(vmem_limit_bytes=32 * 1024 * 1024),
        name="select_rows_and_rotate_queries",
    )(*operands)
    return outs[:half], outs[half:-1], outs[-1]


def gather_kernel(*refs):
    *blocks, out_ref = refs
    width = out_ref.shape[1]
    out_ref[...] = jnp.concatenate([ref[c, :, :width] for ref in blocks for c in range(2)], axis=0)


def gather_rows(width, blocks):
    return pl.pallas_call(
        gather_kernel,
        out_shape=jax.ShapeDtypeStruct((2 * CAP * len(blocks), width), BF16),
        in_specs=[VMEM] * len(blocks),
        out_specs=VMEM,
        compiler_params=pltpu.CompilerParams(vmem_limit_bytes=(2 << 20) + 16 * CAP * len(blocks) * width),
        cost_estimate=pl.CostEstimate(flops=1000000000, bytes_accessed=8 * CAP * len(blocks) * width, transcendentals=0),
        name="gather_rows",
    )(*blocks)


def row_steps(rows):
    return [(i * 128, 64 if i < 4 else 128) for i in range(rows // 128)]


def factor_kernel(act_width, row_out, rounds, blocks, count_ref, *refs):
    here, there = refs[:rounds], refs[rounds : 2 * rounds]
    refs = refs[2 * rounds :]
    near, ready_ref = refs[:blocks], refs[blocks]
    refs = refs[1:]
    act_hbm, grad_hbm, rot_act_hbm, rot_grad_hbm = refs[blocks : blocks + 4]
    right_ref, act_ref, grad_ref, rot_act_ref, rot_grad_ref, sems = refs[blocks + 4 :]
    block, core = lax.axis_index("dp"), lax.axis_index("mp")
    act_block, act_half = act_ref.shape
    grad_block, grad_half = grad_ref.shape
    inverse = 1.0 / count_ref[0].astype(F32)
    contract = (((0,), (0,)), ((), ()))
    copies = []

    def send(src, dst):
        copy = pltpu.make_async_copy(src, dst, sems.at[len(copies)])
        copy.start()
        copies.append(copy)

    def columns(at, width):
        extra = 64 if width % 128 else 0
        start = at - at % 128 if extra else at
        span = pl.ds(pl.multiple_of(start, 128), width + extra)
        late = [ref[c, :, span] for ref in there for c in range(2)]
        rows = jnp.concatenate([ready_ref[:, span]] + late, axis=0)
        if extra:
            rows = jnp.where(at % 128 == 0, rows[:, :width], rows[:, extra:])
        return rows

    def tile(left, right):
        part = lax.dot_general(left, right, contract, preferred_element_type=F32)
        return (part * inverse).astype(BF16)

    right_ref[...] = columns(core * act_half, act_half)
    for first, step in row_steps(act_block):
        left = columns(block * act_block + first, 128)
        for at in range(0, 128, step):
            rows = pl.ds(first + at, step)
            act_ref[rows, :] = tile(left[:, at : at + step], right_ref[...])
            send(act_ref.at[rows], act_hbm.at[rows])

    grad_ref[...] = tile(
        columns(act_width + block * grad_block, grad_block),
        columns(act_width + core * grad_half, grad_half),
    )
    send(grad_ref, grad_hbm)

    act_cols = rot_act_ref.shape[1]
    cols = act_cols + rot_grad_ref.shape[1]
    base = act_width + 2 * grad_half
    for i in range(row_out // 2):
        total = jnp.zeros((2, cols), F32)
        at = base + i * 2 * cols
        for group, c in ((here, 0), (there, 1)):
            for ref in group:
                high = ref[c, :, at : at + cols].astype(F32)
                low = ref[c, :, at + cols : at + 2 * cols].astype(F32)
                total += high + low
        at = base + i * cols
        for ref in near:
            total += ref[0, :, at : at + cols].astype(F32) + ref[1, :, at : at + cols].astype(F32)
        rot_act_ref[2 * i : 2 * i + 2, :] = total[:, :act_cols].astype(BF16)
        rot_grad_ref[2 * i : 2 * i + 2, :] = total[:, act_cols:].astype(BF16)
    send(rot_act_ref, rot_act_hbm)
    send(rot_grad_ref, rot_grad_hbm)
    for copy in copies:
        copy.wait()


def factors(act_width, row_out, act_tile, grad_tile, act_cols, grad_cols, counts, here, there, near, ready):
    rounds, blocks = len(here), len(near)
    shapes = (act_tile, grad_tile, (row_out, act_cols), (row_out, grad_cols))
    return pl.pallas_call(
        functools.partial(factor_kernel, act_width, row_out, rounds, blocks),
        out_shape=tuple(jax.ShapeDtypeStruct(shape, BF16) for shape in shapes),
        in_specs=[SMEM] + [VMEM] * (2 * rounds + blocks + 1),
        out_specs=(HBM,) * 4,
        scratch_shapes=[pltpu.VMEM((2 * CAP * (2 * rounds + blocks), act_tile[1]), BF16)]
        + [pltpu.VMEM(shape, BF16) for shape in shapes]
        + [pltpu.SemaphoreType.DMA((act_tile[0] // 128 + 7,))],
        compiler_params=pltpu.CompilerParams(vmem_limit_bytes=40 * 1024 * 1024),
        name="factor_tiles",
    )(counts, *here, *there, *near, ready)


def local(
    tokens, pseudo, assign, counts, basis_act, basis_grad, queries_act, queries_grad, query_expert
):
    experts, blocks = lax.axis_size("expert"), lax.axis_size("dp")
    toks, d_model = tokens.shape
    slots, hidden = pseudo.shape[1], pseudo.shape[2]
    row_out = query_expert.shape[0] // (experts * blocks)
    order = partner_order(experts, blocks)
    half = len(order[0])
    sends, nears, give = pack(
        order,
        blocks,
        row_out,
        assign.T,
        tokens,
        pseudo.reshape(toks * slots, hidden),
        query_expert.T,
        queries_act,
        queries_grad,
        basis_act[0],
        basis_grad[0],
    )
    swap = [(0, 1), (1, 0)]
    got = lax.ppermute(give, "mp", swap)
    width = d_model + hidden
    nears = [near.at[1, :, :width].set(got[half, :, :width]) for near in nears]
    for dd in range(1, blocks):
        nears[dd] = lax.ppermute(nears[dd], "dp", [(d, d ^ dd) for d in range(blocks)])
    here = []
    for r in reversed(range(half)):
        pairs = [
            ((e * blocks + d) * 2 + m, ((e ^ order[m][r][0]) * blocks + (d ^ order[m][r][1])) * 2 + m)
            for e in range(experts)
            for d in range(blocks)
            for m in range(2)
        ]
        here.append(lax.ppermute(sends[r].at[1].set(got[r]), ("expert", "dp", "mp"), pairs))
    there = [lax.ppermute(rows, "mp", swap) for rows in here]
    act_cov, grad_cov, rot_act, rot_grad = factors(
        d_model,
        row_out,
        (d_model // blocks, d_model // 2),
        (hidden // blocks, hidden // 2),
        basis_act.shape[2],
        basis_grad.shape[2],
        counts,
        here,
        there,
        nears,
        gather_rows(width, here + nears),
    )
    return act_cov[None], grad_cov[None], rot_act, rot_grad


def solution(mesh):
    return jax.shard_map(
        local,
        mesh=mesh,
        in_specs=(
            P(("groups", "expert", "dp", "mp"), None),
            P(("groups", "expert", "dp", "mp"), None, None),
            P(("groups", "expert", "dp", "mp"), None),
            P(("groups", "expert")),
            P(("groups", "expert"), "dp", "mp"),
            P(("groups", "expert"), "dp", "mp"),
            P("groups", "dp"),
            P("groups", "dp"),
            P("groups", None),
        ),
        out_specs=(
            P(("groups", "expert"), "dp", "mp"),
            P(("groups", "expert"), "dp", "mp"),
            P(("groups", "expert", "dp"), "mp"),
            P(("groups", "expert", "dp"), "mp"),
        ),
        check_vma=False,
    )
```
